512 devices in a mesh: gx: 16 (over x, z_hi), gy: 8 (over y, core), gz: 4 (over z_lo).
Axes of the slice: x: 4, y: 4, z: 16 (z_hi: 4, z_lo: 4; z = z_hi * 4 + z_lo), core: 2. Of those that a mesh axis runs over, the one named last changes fastest.
Arguments:
- velocity: float32 [3, 256, 128, 512], P(None, 'gx', 'gy', 'gz'), may hold values from -6 to 6
- stress: float32 [6, 256, 128, 512], P(None, 'gx', 'gy', 'gz'), may hold values from -6 to 6
- memory: float32 [6, 256, 128, 512], P(None, 'gx', 'gy', 'gz'), may hold values from -4 to 4
- lame_lambda: float32 [256, 128, 512], P('gx', 'gy', 'gz'), may hold values from 0.5 to 1.5
- shear_modulus: float32 [256, 128, 512], P('gx', 'gy', 'gz'), may hold values from 0.3 to 1
- buoyancy: float32 [256, 128, 512], P('gx', 'gy', 'gz'), may hold values from 0.5 to 1.5
- anelastic_weight: float32 [256, 128, 512], P('gx', 'gy', 'gz'), may hold values from 0.2 to 1
- decay_table: float32 [8], replicated, may hold values from 0.3 to 0.95
- mech_index: int32 [256, 128, 512], P('gx', 'gy', 'gz'), may hold values from 0 to 7
- surface_depth: int32 [256, 128], P('gx', 'gy'), may hold values from 0 to 3
Outputs:
- velocity_out: float32 [3, 256, 128, 512], P(None, 'gx', 'gy', 'gz')
- stress_out: float32 [6, 256, 128, 512], P(None, 'gx', 'gy', 'gz')
- memory_out: float32 [6, 256, 128, 512], P(None, 'gx', 'gy', 'gz')
The draws below stay inside these ranges and needn't reach their ends.
All inputs are finite; a program needn't handle non-finite values.
Results may differ from the reference program's by a relative error of at most 0.0003.
Values sent between devices are 32-bit elements; how exact they have to be, the bound alone decides.
No kernel may reach another device: no remote copies, remote signals or barrier semaphores. Data moves between devices by JAX's collectives and lax.ppermute only.
A program may use at most 128 MiB of HBM per device.

```python
import jax
import jax.numpy as jnp
from jax import lax

STEPS = 2
MECH = 8
NX = 256
NY = 128
NZ = 512


def plant(entries, rng, least, largest):
    longest = entries.shape.index(max(entries.shape))
    spots = []
    for shift in (0, 1):
        where = [jax.random.randint(jax.random.fold_in(rng, axis), (), 0, length) for axis, length in enumerate(entries.shape)]
        where[longest] = (where[longest] + shift) % entries.shape[longest]
        spots.append(tuple(where))
    return entries.at[spots[0]].set(least).at[spots[1]].set(largest)


def steps_of(rng, shape, pieces, smallest, largest):
    loudness, own = 1.0, jax.random.fold_in(rng, 6)
    for dim, shards_of in pieces:
        heights = jnp.exp(jax.random.uniform(jax.random.fold_in(own, dim), (shards_of,), jnp.float32, smallest / len(pieces), largest / len(pieces)))
        loudness = loudness * jnp.repeat(heights, shape[dim] // shards_of).reshape([-1 if axis == dim else 1 for axis in range(len(shape))])
    return loudness


def centred(rng, shape, width, limit, shards=(), kind=jnp.bfloat16):
    loudness = steps_of(rng, shape, shards, -0.22, 0.18) if shards else 1.0
    drawn = jax.random.normal(rng, shape, jnp.float32) * width * loudness
    return jnp.minimum(jnp.maximum(drawn, -limit), limit).astype(kind)


def setup_inputs(seed: int = 0) -> dict:
    streams_of = jax.random.split(jax.random.key(seed), 11)
    return {
        "velocity": centred(streams_of[0], (3, NX, NY, NZ), 1.0, 6.0, ((1, 16), (2, 8), (3, 4)), jnp.float32),
        "stress": centred(streams_of[1], (6, NX, NY, NZ), 1.0, 6.0, ((1, 16), (2, 8), (3, 4)), jnp.float32),
        "memory": centred(streams_of[2], (6, NX, NY, NZ), 0.5, 4.0, ((1, 16), (2, 8), (3, 4)), jnp.float32),
        "lame_lambda": jnp.clip(0.5 + 1.0 * jax.random.uniform(streams_of[3], (NX, NY, NZ), jnp.float32) ** steps_of(streams_of[3], (NX, NY, NZ), ((0, 16), (1, 8), (2, 4)), -0.2, 0.2), 0.5, 1.5),
        "shear_modulus": jnp.clip(0.3 + 0.7 * jax.random.uniform(streams_of[4], (NX, NY, NZ), jnp.float32) ** steps_of(streams_of[4], (NX, NY, NZ), ((0, 16), (1, 8), (2, 4)), -0.2, 0.2), 0.3, 1.0),
        "buoyancy": jnp.clip(0.5 + 1.0 * jax.random.uniform(streams_of[5], (NX, NY, NZ), jnp.float32) ** steps_of(streams_of[5], (NX, NY, NZ), ((0, 16), (1, 8), (2, 4)), -0.2, 0.2), 0.5, 1.5),
        "anelastic_weight": jnp.clip(0.2 + 0.8 * jax.random.uniform(streams_of[6], (NX, NY, NZ), jnp.float32) ** steps_of(streams_of[6], (NX, NY, NZ), ((0, 16), (1, 8), (2, 4)), -0.2, 0.2), 0.2, 1.0),
        "decay_table": jnp.clip(jax.random.uniform(streams_of[7], (MECH,), jnp.float32, 0.3, 0.95), 0.3, 0.95),
        "mech_index": plant(jax.random.randint(streams_of[8], (NX, NY, NZ), 0, MECH), jax.random.fold_in(streams_of[8], 1), 0, MECH - 1).astype(jnp.int32),
        "surface_depth": plant(jax.random.randint(streams_of[9], (NX, NY), 0, 4), jax.random.fold_in(streams_of[9], 1), 0, 3).astype(jnp.int32),
    }


COEF_NEAR = 9.0 / 8.0
COEF_FAR = -1.0 / 24.0
TIME_STEP = 0.2


def along(padded, axis, offset):
    count = padded.shape[axis] - 4
    return lax.slice_in_dim(padded, 2 + offset, 2 + offset + count, axis=axis)


def forward(padded, axis):
    return COEF_NEAR * (along(padded, axis, 1) - along(padded, axis, 0)) + COEF_FAR * (along(padded, axis, 2) - along(padded, axis, -1))


def backward(padded, axis):
    return COEF_NEAR * (along(padded, axis, 0) - along(padded, axis, -1)) + COEF_FAR * (along(padded, axis, 1) - along(padded, axis, -2))


def crop_other(padded, axis):
    for other in range(3):
        if other != axis:
            padded = lax.slice_in_dim(padded, 2, padded.shape[other] - 2, axis=other)
    return padded


def velocity_update(velocity, buoyancy, fetch):
    scale = TIME_STEP * buoyancy
    vel_x = velocity[0] + scale * (forward(fetch(0, 0), 0) + backward(fetch(3, 1), 1) + backward(fetch(4, 2), 2))
    vel_y = velocity[1] + scale * (backward(fetch(3, 0), 0) + forward(fetch(1, 1), 1) + backward(fetch(5, 2), 2))
    vel_z = velocity[2] + scale * (backward(fetch(4, 0), 0) + backward(fetch(5, 1), 1) + forward(fetch(2, 2), 2))
    return jnp.stack([vel_x, vel_y, vel_z])


def stress_update(padded_vel, stress, memory, lame_lambda, shear_modulus, anelastic_weight, decay_cell, air, surface_cell):
    def fetch(comp, axis):
        return crop_other(padded_vel[comp], axis)
    strain_xx = backward(fetch(0, 0), 0)
    strain_yy = backward(fetch(1, 1), 1)
    strain_zz = backward(fetch(2, 2), 2)
    strain_xy = forward(fetch(0, 1), 1) + forward(fetch(1, 0), 0)
    strain_xz = forward(fetch(0, 2), 2) + forward(fetch(2, 0), 0)
    strain_yz = forward(fetch(1, 2), 2) + forward(fetch(2, 1), 1)
    volume = lame_lambda * (strain_xx + strain_yy + strain_zz)
    rates = jnp.stack([volume + 2.0 * shear_modulus * strain_xx, volume + 2.0 * shear_modulus * strain_yy,
                       volume + 2.0 * shear_modulus * strain_zz, shear_modulus * strain_xy,
                       shear_modulus * strain_xz, shear_modulus * strain_yz])
    memory_new = decay_cell * memory + (1.0 - decay_cell) * anelastic_weight * rates
    stress_new = stress + TIME_STEP * (rates - memory_new)
    keep_all = 1.0 - air
    keep_vertical = keep_all * (1.0 - surface_cell)
    factors = jnp.stack([keep_all, keep_all, keep_vertical, keep_all, keep_vertical, keep_vertical])
    return stress_new * factors, memory_new


def lookup_decay(mech_index, decay_table):
    levels = jnp.arange(decay_table.shape[0], dtype=jnp.int32)
    hits = mech_index[None] == levels[:, None, None, None]
    return jnp.sum(jnp.where(hits, decay_table[:, None, None, None], jnp.float32(0.0)), axis=0)


def pad_all(fields):
    return jnp.pad(fields, ((0, 0), (2, 2), (2, 2), (2, 2)))


def reference(velocity, stress, memory, lame_lambda, shear_modulus, buoyancy, anelastic_weight, decay_table, mech_index, surface_depth):
    decay_cell = lookup_decay(mech_index, decay_table)
    depth_index = jnp.arange(NZ, dtype=jnp.int32)[None, None, :]
    top = surface_depth[:, :, None]
    air = (depth_index < top).astype(jnp.float32)
    surface_cell = (depth_index == top).astype(jnp.float32)
    for step_index in range(STEPS):
        padded_stress = pad_all(stress)
        velocity = velocity_update(velocity, buoyancy, lambda comp, axis: crop_other(padded_stress[comp], axis))
        padded_vel = pad_all(velocity)
        stress, memory = stress_update(padded_vel, stress, memory, lame_lambda, shear_modulus, anelastic_weight, decay_cell, air, surface_cell)
    return velocity, stress, memory
```

```python
import functools

import jax
import jax.numpy as jnp
from jax import lax
from jax.experimental import pallas as pl
from jax.experimental.pallas import tpu as pltpu
from jax.sharding import PartitionSpec as P

STEPS = 2
COEF_NEAR = 9.0 / 8.0
COEF_FAR = -1.0 / 24.0
TIME_STEP = 0.2
AXES = ("gx", "gy", "gz")

STRESS = (
    ((0, "f"), (3, "b"), (4, "b")),
    ((3, "b"), (1, "f"), (5, "b")),
    ((4, "b"), (5, "b"), (2, "f")),
)
VELOCITY = (
    ((0, "b"), (1, "f"), (2, "f")),
    ((1, "b"), (0, "f"), (2, "f")),
    ((2, "b"), (0, "f"), (1, "f")),
)
BEFORE = {"f": (-1,), "b": (-2, -1)}
AFTER = {"f": (0, 1), "b": (0,)}
TAPS = {
    "f": ((1, COEF_NEAR), (0, -COEF_NEAR), (2, COEF_FAR), (-1, -COEF_FAR)),
    "b": ((0, COEF_NEAR), (-1, -COEF_NEAR), (1, COEF_FAR), (-2, -COEF_FAR)),
}


def layers(spec, sides):
    return [(comp, off) for comp, kind in spec for off in sides[kind]]


def weighted(taps):
    a, b, c, d = taps
    return COEF_NEAR * (a - b) + COEF_FAR * (c - d)


class Faces:
    def __init__(self, spec, fields, halos, rows, edges):
        self.spec, self.fields, self.rows, self.edges = spec, fields, rows, edges
        self.xb, self.xa, self.yb, self.ya, self.zb, self.za = halos
        self.nx, self.ny, self.nz = fields.shape[1:]
        self.before = [{k: i for i, k in enumerate(layers(s, BEFORE))} for s in spec]
        self.after = [{k: i for i, k in enumerate(layers(s, AFTER))} for s in spec]

    def prepare(self):
        nx, ny, nz = self.nx, self.ny, self.nz
        for slot, (comp, kind) in enumerate(self.spec[1]):
            for x in range(nx):
                self.rows[slot, x, 8 : 8 + ny, :] = self.fields[comp, x]
                for off in BEFORE[kind]:
                    i = self.before[1][comp, off]
                    self.rows[slot, x, 8 + off : 9 + off, :] = self.yb[i, x : x + 1, :]
                for off in AFTER[kind]:
                    i = self.after[1][comp, off]
                    self.rows[slot, x, 8 + ny + off : 9 + ny + off, :] = self.ya[i, x : x + 1, :]
        got = jnp.concatenate([self.zb[...], self.za[...]], axis=0)
        row = lax.broadcasted_iota(jnp.int32, (16, nz), 0)
        lane = lax.broadcasted_iota(jnp.int32, (16, nz), 1)
        for slot, (comp, kind) in enumerate(self.spec[2]):
            weights = jnp.zeros((16, nz), jnp.float32)
            for shift, weight in TAPS[kind]:
                for off in BEFORE[kind]:
                    at = off - shift
                    if 0 <= at < nz:
                        hit = (row == self.before[2][comp, off]) & (lane == at)
                        weights = weights + jnp.where(hit, weight, 0.0)
                for off in AFTER[kind]:
                    at = nz + off - shift
                    if 0 <= at < nz:
                        hit = (row == 8 + self.after[2][comp, off]) & (lane == at)
                        weights = weights + jnp.where(hit, weight, 0.0)
            self.edges[slot] = lax.dot_general(
                got,
                weights,
                (((0,), (0,)), ((), ())),
                precision=lax.Precision.HIGHEST,
                preferred_element_type=jnp.float32,
            )

    def dx(self, comp, x):
        kind = dict(self.spec[0])[comp]

        def plane(at):
            if at < 0:
                return self.xb[self.before[0][comp, at]]
            if at >= self.nx:
                return self.xa[self.after[0][comp, at - self.nx]]
            return self.fields[comp, at]

        return weighted([plane(x + off) for off, _ in TAPS[kind]])

    def dy(self, comp, x):
        slot = [c for c, _ in self.spec[1]].index(comp)
        kind = self.spec[1][slot][1]
        return weighted(
            [self.rows[slot, x, 8 + off : 8 + off + self.ny, :] for off, _ in TAPS[kind]]
        )

    def dz(self, comp, x):
        slot = [c for c, _ in self.spec[2]].index(comp)
        kind = self.spec[2][slot][1]
        here = self.fields[comp, x]
        lane = lax.broadcasted_iota(jnp.int32, (1, self.nz), 1)
        total = self.edges[slot, x * self.ny : (x + 1) * self.ny, :]
        for off, weight in TAPS[kind]:
            if off == 0:
                total = total + weight * here
            else:
                inside = (lane + off >= 0) & (lane + off < self.nz)
                moved = pltpu.roll(here, (-off) % self.nz, 1)
                total = total + jnp.where(inside, weight, 0.0) * moved
        return total


def pack(spec, fields, up, down):
    nx, ny, nz = fields.shape[1:]
    xu, yu, zu = up
    xd, yd, zd = down
    for i, (comp, off) in enumerate(layers(spec[0], BEFORE)):
        xu[i] = fields[comp, nx + off]
    for i, (comp, off) in enumerate(layers(spec[0], AFTER)):
        xd[i] = fields[comp, off]
    for i, (comp, off) in enumerate(layers(spec[1], BEFORE)):
        yu[i] = fields[comp, :, ny + off, :]
    for i, (comp, off) in enumerate(layers(spec[1], AFTER)):
        yd[i] = fields[comp, :, off, :]
    row = lax.broadcasted_iota(jnp.int32, (16, nz), 0)
    lane = lax.broadcasted_iota(jnp.int32, (16, nz), 1)
    before, after = layers(spec[2], BEFORE), layers(spec[2], AFTER)
    total = None
    for comp, _ in spec[2]:
        pick = jnp.zeros((16, nz), jnp.float32)
        for i, (c, off) in enumerate(before):
            if c == comp:
                pick = jnp.where((row == i) & (lane == nz + off), 1.0, pick)
        for i, (c, off) in enumerate(after):
            if c == comp:
                pick = jnp.where((row == 8 + i) & (lane == off), 1.0, pick)
        part = lax.dot_general(
            pick,
            fields[comp].reshape(nx * ny, nz),
            (((1,), (1,)), ((), ())),
            precision=lax.Precision.HIGHEST,
            preferred_element_type=jnp.float32,
        )
        total = part if total is None else total + part
    zu[...] = total[:8]
    zd[...] = total[8:]


def first_kernel(stress, xu, xd, yu, yd, zu, zd):
    pack(STRESS, stress, (xu, yu, zu), (xd, yd, zd))


def velocity_kernel(send, *refs):
    stress, velocity, buoyancy = refs[:3]
    out = refs[9]
    faces = Faces(STRESS, stress, refs[3:9], refs[-2], refs[-1])
    faces.prepare()
    for x in range(velocity.shape[1]):
        scale = TIME_STEP * buoyancy[x]
        out[0, x] = velocity[0, x] + scale * (faces.dx(0, x) + faces.dy(3, x) + faces.dz(4, x))
        out[1, x] = velocity[1, x] + scale * (faces.dx(3, x) + faces.dy(1, x) + faces.dz(5, x))
        out[2, x] = velocity[2, x] + scale * (faces.dx(4, x) + faces.dy(5, x) + faces.dz(2, x))
    if send:
        xu, xd, yu, yd, zu, zd = refs[10:16]
        pack(VELOCITY, out, (xu, yu, zu), (xd, yd, zd))


def stress_kernel(send, *refs):
    velocity, stress, memory, lam, shear, weight, mech, top_ref, first, table = refs[:10]
    out, kept = refs[16:18]
    faces = Faces(VELOCITY, velocity, refs[10:16], refs[-2], refs[-1])
    faces.prepare()
    nx, ny, nz = lam.shape
    tops = top_ref[...].astype(jnp.float32).T
    depth = (first[0] + lax.broadcasted_iota(jnp.int32, (1, nz), 1)).astype(jnp.float32)
    for x in range(nx):
        decay = jnp.zeros((ny, nz), jnp.float32)
        for level in range(table.shape[0]):
            decay = jnp.where(mech[x] == level, table[level], decay)
        gain = (1.0 - decay) * weight[x]
        top = tops[:, x : x + 1]
        solid = depth >= top
        below = depth > top
        xx, yy, zz = faces.dx(0, x), faces.dy(1, x), faces.dz(2, x)
        volume = lam[x] * (xx + yy + zz)
        double = 2.0 * shear[x]
        rates = (
            volume + double * xx,
            volume + double * yy,
            volume + double * zz,
            shear[x] * (faces.dy(0, x) + faces.dx(1, x)),
            shear[x] * (faces.dz(0, x) + faces.dx(2, x)),
            shear[x] * (faces.dz(1, x) + faces.dy(2, x)),
        )
        for comp, rate in enumerate(rates):
            new = decay * memory[comp, x] + gain * rate
            kept[comp, x] = new
            keep = below if comp in (2, 4, 5) else solid
            out[comp, x] = jnp.where(keep, stress[comp, x] + TIME_STEP * (rate - new), 0.0)
    if send:
        xu, xd, yu, yd, zu, zd = refs[18:24]
        pack(STRESS, out, (xu, yu, zu), (xd, yd, zd))


def face_shapes(spec, nx, ny, nz):
    shapes = []
    for sides in (BEFORE, AFTER):
        shapes.append((len(layers(spec[0], sides)), ny, nz))
        shapes.append((len(layers(spec[1], sides)), nx, nz))
        shapes.append((8, nx * ny))
    xu, yu, zu, xd, yd, zd = [jax.ShapeDtypeStruct(s, jnp.float32) for s in shapes]
    return [xu, xd, yu, yd, zu, zd]


def call(body, outs, operands, scalars=(), scratch=()):
    vmem = pl.BlockSpec(memory_space=pltpu.VMEM)
    smem = pl.BlockSpec(memory_space=pltpu.SMEM)
    return pl.pallas_call(
        body,
        out_shape=outs,
        in_specs=[smem if i in scalars else vmem for i in range(len(operands))],
        out_specs=[vmem] * len(outs),
        scratch_shapes=list(scratch),
        compiler_params=pltpu.CompilerParams(vmem_limit_bytes=24 * 1024 * 1024),
    )(*operands)


def exchange(faces):
    got = []
    for i, face in enumerate(faces):
        axis = AXES[i // 2]
        peers = lax.axis_size(axis)
        pairs = [(j, j + 1) for j in range(peers - 1)]
        if i % 2:
            pairs = [(b, a) for a, b in pairs]
        got.append(lax.ppermute(face, axis, pairs))
    return got


def shards(
    velocity,
    stress,
    memory,
    lame_lambda,
    shear_modulus,
    buoyancy,
    anelastic_weight,
    decay_table,
    mech_index,
    surface_depth,
):
    nx, ny, nz = lame_lambda.shape
    first = (lax.axis_index("gz") * nz).astype(jnp.int32).reshape(1)
    like = lambda a: jax.ShapeDtypeStruct(a.shape, a.dtype)
    scratch = (
        pltpu.VMEM((3, nx, ny + 16, nz), jnp.float32),
        pltpu.VMEM((3, nx * ny, nz), jnp.float32),
    )
    stress_faces = face_shapes(STRESS, nx, ny, nz)
    velocity_faces = face_shapes(VELOCITY, nx, ny, nz)
    faces = call(first_kernel, stress_faces, [stress])
    for step in range(STEPS):
        halos = exchange(faces)
        velocity, *faces = call(
            functools.partial(velocity_kernel, True),
            [like(velocity)] + velocity_faces,
            [stress, velocity, buoyancy, *halos],
            scratch=scratch,
        )
        halos = exchange(faces)
        send = step < STEPS - 1
        stress, memory, *faces = call(
            functools.partial(stress_kernel, send),
            [like(stress), like(memory)] + (stress_faces if send else []),
            [
                velocity,
                stress,
                memory,
                lame_lambda,
                shear_modulus,
                anelastic_weight,
                mech_index,
                surface_depth,
                first,
                decay_table,
                *halos,
            ],
            scalars=(8, 9),
            scratch=scratch,
        )
    return (velocity, stress, memory)


def solution(mesh):
    fields = P(None, *AXES)
    cells = P(*AXES)
    return jax.shard_map(
        shards,
        mesh=mesh,
        in_specs=(fields,) * 3 + (cells,) * 4 + (P(), cells, P("gx", "gy")),
        out_specs=(fields,) * 3,
        check_vma=False,
    )
```

```python
import functools

import jax
import jax.numpy as jnp
from jax import lax
from jax.experimental import pallas as pl
from jax.experimental.pallas import tpu as pltpu
from jax.sharding import PartitionSpec as P

STEPS = 2
COEF_NEAR = 9.0 / 8.0
COEF_FAR = -1.0 / 24.0
TIME_STEP = 0.2
AXES = ("gx", "gy", "gz")

STRESS = (
    ((0, "f"), (3, "b"), (4, "b")),
    ((3, "b"), (1, "f"), (5, "b")),
    ((4, "b"), (5, "b"), (2, "f")),
)
VELOCITY = (
    ((0, "b"), (1, "f"), (2, "f")),
    ((1, "b"), (0, "f"), (2, "f")),
    ((2, "b"), (0, "f"), (1, "f")),
)
BEFORE = {"f": (-1,), "b": (-2, -1)}
AFTER = {"f": (0, 1), "b": (0,)}
TAPS = {
    "f": ((1, COEF_NEAR), (0, -COEF_NEAR), (2, COEF_FAR), (-1, -COEF_FAR)),
    "b": ((0, COEF_NEAR), (-1, -COEF_NEAR), (1, COEF_FAR), (-2, -COEF_FAR)),
}

FACE = 5
INNER = FACE + 1
GIVEN = INNER + FACE
TAKEN = 2 * FACE + 2


def layers(spec, sides):
    return [(comp, off) for comp, kind in spec for off in sides[kind]]


def weighted(taps):
    a, b, c, d = taps
    return COEF_NEAR * (a - b) + COEF_FAR * (c - d)


class Faces:
    def __init__(self, spec, fields, core, pair, spread, outer, rows, edges):
        self.spec, self.fields, self.rows, self.edges = spec, fields, rows, edges
        self.core, self.pair, self.spread, self.outer = core, pair, spread, outer
        self.nx, self.ny, self.nz = fields.shape[1:]
        self.before = [{k: i for i, k in enumerate(layers(s, BEFORE))} for s in spec]
        self.after = [{k: i for i, k in enumerate(layers(s, AFTER))} for s in spec]

    def prepare(self):
        nx, ny, nz = self.nx, self.ny, self.nz
        for slot, (comp, kind) in enumerate(self.spec[1]):
            for x in range(nx):
                self.rows[slot, x, 8 : 8 + ny, :] = self.fields[comp, x]

        def beside(before, after):
            for slot, (comp, kind) in enumerate(self.spec[1]):
                for x in range(nx):
                    for off in BEFORE[kind]:
                        i = self.before[1][comp, off]
                        self.rows[slot, x, 8 + off : 9 + off, :] = before(i, x)
                    for off in AFTER[kind]:
                        i = self.after[1][comp, off]
                        self.rows[slot, x, 8 + ny + off : 9 + ny + off, :] = after(i, x)

        outer = lambda i, x: self.outer[i, x : x + 1, :]

        @pl.when(self.core == 0)
        def _():
            beside(outer, lambda i, x: self.pair[GIVEN + INNER + i, x : x + 1, :])

        @pl.when(self.core == 1)
        def _():
            beside(lambda i, x: self.pair[INNER + i, x : x + 1, :], outer)

        ends = [self.spread[side * TAKEN + 2 * FACE + self.core] for side in (0, 1)]
        got = jnp.concatenate([jnp.concatenate([e[:8], e[8:]], axis=1) for e in ends], axis=0)
        row = lax.broadcasted_iota(jnp.int32, (16, nz), 0)
        lane = lax.broadcasted_iota(jnp.int32, (16, nz), 1)
        for slot, (comp, kind) in enumerate(self.spec[2]):
            weights = jnp.zeros((16, nz), jnp.float32)
            for shift, weight in TAPS[kind]:
                for off in BEFORE[kind]:
                    at = off - shift
                    if 0 <= at < nz:
                        hit = (row == self.before[2][comp, off]) & (lane == at)
                        weights = weights + jnp.where(hit, weight, 0.0)
                for off in AFTER[kind]:
                    at = nz + off - shift
                    if 0 <= at < nz:
                        hit = (row == 8 + self.after[2][comp, off]) & (lane == at)
                        weights = weights + jnp.where(hit, weight, 0.0)
            self.edges[slot] = lax.dot_general(
                got,
                weights,
                (((0,), (0,)), ((), ())),
                precision=lax.Precision.HIGHEST,
                preferred_element_type=jnp.float32,
            )

    def dx(self, comp, x):
        kind = dict(self.spec[0])[comp]

        def plane(at):
            if at < 0:
                return self.spread[self.core * FACE + self.before[0][comp, at]]
            if at >= self.nx:
                return self.spread[TAKEN + self.core * FACE + self.after[0][comp, at - self.nx]]
            return self.fields[comp, at]

        return weighted([plane(x + off) for off, _ in TAPS[kind]])

    def dy(self, comp, x):
        slot = [c for c, _ in self.spec[1]].index(comp)
        kind = self.spec[1][slot][1]
        return weighted(
            [self.rows[slot, x, 8 + off : 8 + off + self.ny, :] for off, _ in TAPS[kind]]
        )

    def dz(self, comp, x):
        slot = [c for c, _ in self.spec[2]].index(comp)
        kind = self.spec[2][slot][1]
        here = self.fields[comp, x]
        lane = lax.broadcasted_iota(jnp.int32, (1, self.nz), 1)
        total = self.edges[slot, x * self.ny : (x + 1) * self.ny, :]
        for off, weight in TAPS[kind]:
            if off == 0:
                total = total + weight * here
            else:
                inside = (lane + off >= 0) & (lane + off < self.nz)
                moved = pltpu.roll(here, (-off) % self.nz, 1)
                total = total + jnp.where(inside, weight, 0.0) * moved
        return total


def pack(spec, fields, core, own, given):
    nx, ny, nz = fields.shape[1:]
    row = lax.broadcasted_iota(jnp.int32, (16, nz), 0)
    lane = lax.broadcasted_iota(jnp.int32, (16, nz), 1)
    before, after = layers(spec[2], BEFORE), layers(spec[2], AFTER)
    total = None
    for comp, _ in spec[2]:
        pick = jnp.zeros((16, nz), jnp.float32)
        for i, (c, off) in enumerate(before):
            if c == comp:
                pick = jnp.where((row == i) & (lane == nz + off), 1.0, pick)
        for i, (c, off) in enumerate(after):
            if c == comp:
                pick = jnp.where((row == 8 + i) & (lane == off), 1.0, pick)
        part = lax.dot_general(
            pick,
            fields[comp].reshape(nx * ny, nz),
            (((1,), (1,)), ((), ())),
            precision=lax.Precision.HIGHEST,
            preferred_element_type=jnp.float32,
        )
        total = part if total is None else total + part
    half = nx * ny // 2
    ends = [jnp.concatenate([t[:, :half], t[:, half:]], axis=0) for t in (total[:8], total[8:])]

    def write(up, down, inner_up):
        for ref, sides in ((up, BEFORE), (down, AFTER)):
            for i, (comp, off) in enumerate(layers(spec[0], sides)):
                ref[i] = fields[comp, nx + off if sides is BEFORE else off]
        up[FACE] = ends[0]
        down[FACE] = ends[1]
        inner, outer = (BEFORE, AFTER) if inner_up else (AFTER, BEFORE)
        for ref, sides in ((given, inner), (own, outer)):
            for i, (comp, off) in enumerate(layers(spec[1], sides)):
                ref[INNER + i] = fields[comp, :, ny + off if sides is BEFORE else off, :]

    @pl.when(core == 0)
    def _():
        write(own, given, True)

    @pl.when(core == 1)
    def _():
        write(given, own, False)


def first_kernel(core, stress, own, given):
    pack(STRESS, stress, core[0], own, given)


def gather_kernel(core, own, pair, along_x, along_y, along_z):
    here = core[0]
    there = 1 - here
    other = there * GIVEN
    along_x[pl.ds(here * FACE, FACE)] = own[:FACE]
    along_x[pl.ds(there * FACE, FACE)] = pair[pl.ds(other, FACE)]
    along_z[here] = own[FACE]
    along_z[there] = pair[other + FACE]
    along_y[...] = own[INNER:]


def join_kernel(along_x, along_z, taken):
    taken[: 2 * FACE] = along_x[...]
    taken[2 * FACE :] = along_z[...]


def velocity_kernel(*refs):
    core, stress, velocity, buoyancy, pair, spread, outer, out = refs[:8]
    faces = Faces(STRESS, stress, core[0], pair, spread, outer, refs[-2], refs[-1])
    faces.prepare()
    for x in range(velocity.shape[1]):
        scale = TIME_STEP * buoyancy[x]
        out[0, x] = velocity[0, x] + scale * (faces.dx(0, x) + faces.dy(3, x) + faces.dz(4, x))
        out[1, x] = velocity[1, x] + scale * (faces.dx(3, x) + faces.dy(1, x) + faces.dz(5, x))
        out[2, x] = velocity[2, x] + scale * (faces.dx(4, x) + faces.dy(5, x) + faces.dz(2, x))
    pack(VELOCITY, out, core[0], *refs[8:10])


def stress_kernel(send, *refs):
    core, first, table, velocity, stress, memory, lam, shear, weight, mech, top_ref = refs[:11]
    pair, spread, outer, out, kept = refs[11:16]
    faces = Faces(VELOCITY, velocity, core[0], pair, spread, outer, refs[-2], refs[-1])
    faces.prepare()
    nx, ny, nz = lam.shape
    tops = top_ref[...].astype(jnp.float32).T
    depth = (first[0] + lax.broadcasted_iota(jnp.int32, (1, nz), 1)).astype(jnp.float32)
    for x in range(nx):
        decay = jnp.zeros((ny, nz), jnp.float32)
        for level in range(table.shape[0]):
            decay = jnp.where(mech[x] == level, table[level], decay)
        gain = (1.0 - decay) * weight[x]
        top = tops[:, x : x + 1]
        solid = depth >= top
        below = depth > top
        xx, yy, zz = faces.dx(0, x), faces.dy(1, x), faces.dz(2, x)
        volume = lam[x] * (xx + yy + zz)
        double = 2.0 * shear[x]
        rates = (
            volume + double * xx,
            volume + double * yy,
            volume + double * zz,
            shear[x] * (faces.dy(0, x) + faces.dx(1, x)),
            shear[x] * (faces.dz(0, x) + faces.dx(2, x)),
            shear[x] * (faces.dz(1, x) + faces.dy(2, x)),
        )
        for comp, rate in enumerate(rates):
            new = decay * memory[comp, x] + gain * rate
            kept[comp, x] = new
            keep = below if comp in (2, 4, 5) else solid
            out[comp, x] = jnp.where(keep, stress[comp, x] + TIME_STEP * (rate - new), 0.0)
    if send:
        pack(STRESS, out, core[0], *refs[16:18])


def call(body, outs, operands, scalars=1, scratch=()):
    vmem = pl.BlockSpec(memory_space=pltpu.VMEM)
    smem = pl.BlockSpec(memory_space=pltpu.SMEM)
    return pl.pallas_call(
        body,
        out_shape=outs,
        in_specs=[smem if i < scalars else vmem for i in range(len(operands))],
        out_specs=[vmem] * len(outs),
        scratch_shapes=list(scratch),
        compiler_params=pltpu.CompilerParams(vmem_limit_bytes=24 * 1024 * 1024),
    )(*operands)


def exchange(core, own, given):
    plane = own.shape[1:]
    planes = lambda n: jax.ShapeDtypeStruct((n,) + plane, own.dtype)
    gx, gy, gz = [lax.axis_size(axis) for axis in AXES]
    cores = [[j, j + 1] for j in range(0, gy, 2)]
    pair = lax.all_gather(given, "gy", axis=0, tiled=True, axis_index_groups=cores)
    along_x, along_y, along_z = call(
        gather_kernel, [planes(2 * FACE), planes(FACE), planes(2)], [core, own, pair]
    )
    to_x, to_z = [], []
    for j in range(gy):
        step = 1 - 2 * (j % 2)
        to_x += [(i * gy + j, (i + step) * gy + j) for i in range(gx) if 0 <= i + step < gx]
        to_z += [(j * gz + k, j * gz + k + step) for k in range(gz) if 0 <= k + step < gz]
    to_y = [(j, j + 1) for j in range(1, gy - 1, 2)] + [(j + 1, j) for j in range(1, gy - 1, 2)]
    got_x = lax.ppermute(along_x, ("gx", "gy"), to_x)
    got_z = lax.ppermute(along_z, ("gy", "gz"), to_z)
    outer = lax.ppermute(along_y, "gy", to_y)
    (taken,) = call(join_kernel, [planes(TAKEN)], [got_x, got_z], scalars=0)
    spread = lax.all_gather(taken, "gy", axis=0, tiled=True, axis_index_groups=cores)
    return pair, spread, outer


def shards(
    velocity,
    stress,
    memory,
    lame_lambda,
    shear_modulus,
    buoyancy,
    anelastic_weight,
    decay_table,
    mech_index,
    surface_depth,
):
    nx, ny, nz = lame_lambda.shape
    core = (lax.axis_index("gy") % 2).astype(jnp.int32).reshape(1)
    first = (lax.axis_index("gz") * nz).astype(jnp.int32).reshape(1)
    like = lambda a: jax.ShapeDtypeStruct(a.shape, a.dtype)
    packed = [jax.ShapeDtypeStruct((GIVEN, ny, nz), jnp.float32)] * 2
    scratch = (
        pltpu.VMEM((3, nx, ny + 16, nz), jnp.float32),
        pltpu.VMEM((3, nx * ny, nz), jnp.float32),
    )
    own, given = call(first_kernel, packed, [core, stress])
    for step in range(STEPS):
        velocity, own, given = call(
            velocity_kernel,
            [like(velocity)] + packed,
            [core, stress, velocity, buoyancy, *exchange(core, own, given)],
            scratch=scratch,
        )
        send = step < STEPS - 1
        stress, memory, *rest = call(
            functools.partial(stress_kernel, send),
            [like(stress), like(memory)] + (packed if send else []),
            [
                core,
                first,
                decay_table,
                velocity,
                stress,
                memory,
                lame_lambda,
                shear_modulus,
                anelastic_weight,
                mech_index,
                surface_depth,
                *exchange(core, own, given),
            ],
            scalars=3,
            scratch=scratch,
        )
        if send:
            own, given = rest
    return (velocity, stress, memory)


def solution(mesh):
    fields = P(None, *AXES)
    cells = P(*AXES)
    return jax.shard_map(
        shards,
        mesh=mesh,
        in_specs=(fields,) * 3 + (cells,) * 4 + (P(), cells, P("gx", "gy")),
        out_specs=(fields,) * 3,
        check_vma=False,
    )
```

```python
import jax
import jax.numpy as jnp
from jax import lax
from jax.experimental import pallas as pl
from jax.experimental.pallas import tpu as pltpu
from jax.sharding import PartitionSpec as P

STEPS = 2
COEF_NEAR = 9.0 / 8.0
COEF_FAR = -1.0 / 24.0
TIME_STEP = 0.2
AXES = ("gx", "gy", "gz")

STRESS = (
    ((0, "f"), (3, "b"), (4, "b")),
    ((3, "b"), (1, "f"), (5, "b")),
    ((4, "b"), (5, "b"), (2, "f")),
)
VELOCITY = (
    ((0, "b"), (1, "f"), (2, "f")),
    ((1, "b"), (0, "f"), (2, "f")),
    ((2, "b"), (0, "f"), (1, "f")),
)
BEFORE = {"f": (-1,), "b": (-2, -1)}
AFTER = {"f": (0, 1), "b": (0,)}
TAPS = {
    "f": ((1, COEF_NEAR), (0, -COEF_NEAR), (2, COEF_FAR), (-1, -COEF_FAR)),
    "b": ((0, COEF_NEAR), (-1, -COEF_NEAR), (1, COEF_FAR), (-2, -COEF_FAR)),
}

FACE = 5
GIVEN = 1 + FACE
TAKEN = 2 * FACE + 2


def edge_planes(nx):
    return {0: 0, 1: 1, nx - 2: 2, nx - 1: 3}


def layers(spec, sides):
    return [(comp, off) for comp, kind in spec for off in sides[kind]]


def weighted(taps):
    a, b, c, d = taps
    return COEF_NEAR * (a - b) + COEF_FAR * (c - d)


class Faces:
    def __init__(self, spec, fields, planes, core, pair, spread, outer, rows, edges):
        self.spec, self.fields, self.rows, self.edges = spec, fields, rows, edges
        self.planes = planes
        self.core, self.pair, self.spread, self.outer = core, pair, spread, outer
        self.nx, self.ny, self.nz = fields.shape[1:]
        self.before = [{k: i for i, k in enumerate(layers(s, BEFORE))} for s in spec]
        self.after = [{k: i for i, k in enumerate(layers(s, AFTER))} for s in spec]

    def prepare(self):
        nx, ny, nz = self.nx, self.ny, self.nz
        for slot, (comp, kind) in enumerate(self.spec[1]):
            for x in self.planes:
                self.rows[slot, x, 8 : 8 + ny, :] = self.fields[comp, x]

        def beside(before, after):
            for slot, (comp, kind) in enumerate(self.spec[1]):
                for x in self.planes:
                    for off in BEFORE[kind]:
                        i = self.before[1][comp, off]
                        self.rows[slot, x, 8 + off : 9 + off, :] = before(i, x)
                    for off in AFTER[kind]:
                        i = self.after[1][comp, off]
                        self.rows[slot, x, 8 + ny + off : 9 + ny + off, :] = after(i, x)

        outer = lambda i, x: self.outer[i, x : x + 1, :]

        @pl.when(self.core == 0)
        def _():
            beside(outer, lambda i, x: self.pair[GIVEN + 1 + i, x : x + 1, :])

        @pl.when(self.core == 1)
        def _():
            beside(lambda i, x: self.pair[1 + i, x : x + 1, :], outer)

        ends = [self.spread[side * TAKEN + 2 * FACE + self.core] for side in (0, 1)]
        got = jnp.concatenate([jnp.concatenate([e[:8], e[8:]], axis=1) for e in ends], axis=0)
        row = lax.broadcasted_iota(jnp.int32, (16, nz), 0)
        lane = lax.broadcasted_iota(jnp.int32, (16, nz), 1)
        for slot, (comp, kind) in enumerate(self.spec[2]):
            weights = jnp.zeros((16, nz), jnp.float32)
            for shift, weight in TAPS[kind]:
                for off in BEFORE[kind]:
                    at = off - shift
                    if 0 <= at < nz:
                        hit = (row == self.before[2][comp, off]) & (lane == at)
                        weights = weights + jnp.where(hit, weight, 0.0)
                for off in AFTER[kind]:
                    at = nz + off - shift
                    if 0 <= at < nz:
                        hit = (row == 8 + self.after[2][comp, off]) & (lane == at)
                        weights = weights + jnp.where(hit, weight, 0.0)
            for start, stop in self.columns():
                self.edges[slot, start:stop, :] = lax.dot_general(
                    got[:, start:stop],
                    weights,
                    (((0,), (0,)), ((), ())),
                    precision=lax.Precision.HIGHEST,
                    preferred_element_type=jnp.float32,
                )

    def columns(self):
        if len(self.planes) > 4:
            return [(0, self.nx * self.ny)]
        return [(0, 2 * self.ny), ((self.nx - 2) * self.ny, self.nx * self.ny)]

    def dx(self, comp, x):
        kind = dict(self.spec[0])[comp]

        def plane(at):
            if at < 0:
                return self.spread[self.core * FACE + self.before[0][comp, at]]
            if at >= self.nx:
                return self.spread[TAKEN + self.core * FACE + self.after[0][comp, at - self.nx]]
            return self.fields[comp, at]

        return weighted([plane(x + off) for off, _ in TAPS[kind]])

    def dy(self, comp, x):
        slot = [c for c, _ in self.spec[1]].index(comp)
        kind = self.spec[1][slot][1]
        return weighted(
            [self.rows[slot, x, 8 + off : 8 + off + self.ny, :] for off, _ in TAPS[kind]]
        )

    def dz(self, comp, x):
        slot = [c for c, _ in self.spec[2]].index(comp)
        kind = self.spec[2][slot][1]
        here = self.fields[comp, x]
        lane = lax.broadcasted_iota(jnp.int32, (1, self.nz), 1)
        total = self.edges[slot, x * self.ny : (x + 1) * self.ny, :]
        for off, weight in TAPS[kind]:
            if off == 0:
                total = total + weight * here
            else:
                inside = (lane + off >= 0) & (lane + off < self.nz)
                moved = pltpu.roll(here, (-off) % self.nz, 1)
                total = total + jnp.where(inside, weight, 0.0) * moved
        return total


def pack_x(spec, fields, place, nx, core, own, given):
    def write(up, down):
        for i, (comp, off) in enumerate(layers(spec[0], BEFORE)):
            up[i] = fields[comp, place[nx + off]]
        for i, (comp, off) in enumerate(layers(spec[0], AFTER)):
            down[i] = fields[comp, place[off]]

    @pl.when(core == 0)
    def _():
        write(own, given)

    @pl.when(core == 1)
    def _():
        write(given, own)


def pack_yz(spec, fields, core, own, given):
    nx, ny, nz = fields.shape[1:]
    row = lax.broadcasted_iota(jnp.int32, (16, nz), 0)
    lane = lax.broadcasted_iota(jnp.int32, (16, nz), 1)
    before, after = layers(spec[2], BEFORE), layers(spec[2], AFTER)
    total = None
    for comp, _ in spec[2]:
        pick = jnp.zeros((16, nz), jnp.float32)
        for i, (c, off) in enumerate(before):
            if c == comp:
                pick = jnp.where((row == i) & (lane == nz + off), 1.0, pick)
        for i, (c, off) in enumerate(after):
            if c == comp:
                pick = jnp.where((row == 8 + i) & (lane == off), 1.0, pick)
        part = lax.dot_general(
            pick,
            fields[comp].reshape(nx * ny, nz),
            (((1,), (1,)), ((), ())),
            precision=lax.Precision.HIGHEST,
            preferred_element_type=jnp.float32,
        )
        total = part if total is None else total + part
    half = nx * ny // 2
    ends = [jnp.concatenate([t[:, :half], t[:, half:]], axis=0) for t in (total[:8], total[8:])]

    def write(up, down, inner, outer):
        up[0] = ends[0]
        down[0] = ends[1]
        for ref, sides in ((given, inner), (own, outer)):
            for i, (comp, off) in enumerate(layers(spec[1], sides)):
                ref[1 + i] = fields[comp, :, ny + off if sides is BEFORE else off, :]

    @pl.when(core == 0)
    def _():
        write(own, given, BEFORE, AFTER)

    @pl.when(core == 1)
    def _():
        write(given, own, AFTER, BEFORE)


def first_x_kernel(core, stress, own, given):
    nx = stress.shape[1]
    pack_x(STRESS, stress, {x: x for x in range(nx)}, nx, core[0], own, given)


def first_yz_kernel(core, stress, behind, own, given):
    pack_yz(STRESS, stress, core[0], own, given)


def gather_x_kernel(core, own, pair, along_x):
    here = core[0]
    there = 1 - here
    along_x[pl.ds(here * FACE, FACE)] = own[...]
    along_x[pl.ds(there * FACE, FACE)] = pair[pl.ds(there * FACE, FACE)]


def gather_yz_kernel(core, own, pair, along_y, along_z):
    here = core[0]
    there = 1 - here
    along_z[here] = own[0]
    along_z[there] = pair[there * GIVEN]
    along_y[...] = own[1:]


def join_kernel(along_x, along_z, taken):
    taken[: 2 * FACE] = along_x[...]
    taken[2 * FACE :] = along_z[...]


def velocity_planes(faces, velocity, buoyancy, write):
    for x in faces.planes:
        scale = TIME_STEP * buoyancy[x]
        write(0, x, velocity[0, x] + scale * (faces.dx(0, x) + faces.dy(3, x) + faces.dz(4, x)))
        write(1, x, velocity[1, x] + scale * (faces.dx(3, x) + faces.dy(1, x) + faces.dz(5, x)))
        write(2, x, velocity[2, x] + scale * (faces.dx(4, x) + faces.dy(5, x) + faces.dz(2, x)))


def velocity_edge_kernel(core, stress, velocity, buoyancy, pair, spread, outer, *refs):
    out, own, given, rows, edges = refs
    nx = stress.shape[1]
    place = edge_planes(nx)
    faces = Faces(STRESS, stress, list(place), core[0], pair, spread, outer, rows, edges)
    faces.prepare()

    def write(comp, x, value):
        out[comp, place[x]] = value

    velocity_planes(faces, velocity, buoyancy, write)
    pack_x(VELOCITY, out, place, nx, core[0], own, given)


def velocity_rest_kernel(core, stress, velocity, buoyancy, pair, spread, outer, *refs):
    edge, behind, out, own, given, rows, edges = refs
    nx = stress.shape[1]
    place = edge_planes(nx)
    for x, at in place.items():
        for comp in range(3):
            out[comp, x] = edge[comp, at]
    inner = [x for x in range(nx) if x not in place]
    faces = Faces(STRESS, stress, inner, core[0], pair, spread, outer, rows, edges)
    faces.prepare()

    def write(comp, x, value):
        out[comp, x] = value

    velocity_planes(faces, velocity, buoyancy, write)
    pack_yz(VELOCITY, out, core[0], own, given)


def stress_planes(faces, first, table, stress, memory, cells, write):
    lam, shear, weight, mech, top_ref = cells
    nx, ny, nz = lam.shape
    tops = top_ref[...].astype(jnp.float32).T
    depth = (first[0] + lax.broadcasted_iota(jnp.int32, (1, nz), 1)).astype(jnp.float32)
    for x in faces.planes:
        decay = jnp.zeros((ny, nz), jnp.float32)
        for level in range(table.shape[0]):
            decay = jnp.where(mech[x] == level, table[level], decay)
        gain = (1.0 - decay) * weight[x]
        top = tops[:, x : x + 1]
        solid = depth >= top
        below = depth > top
        xx, yy, zz = faces.dx(0, x), faces.dy(1, x), faces.dz(2, x)
        volume = lam[x] * (xx + yy + zz)
        double = 2.0 * shear[x]
        rates = (
            volume + double * xx,
            volume + double * yy,
            volume + double * zz,
            shear[x] * (faces.dy(0, x) + faces.dx(1, x)),
            shear[x] * (faces.dz(0, x) + faces.dx(2, x)),
            shear[x] * (faces.dz(1, x) + faces.dy(2, x)),
        )
        for comp, rate in enumerate(rates):
            new = decay * memory[comp, x] + gain * rate
            keep = below if comp in (2, 4, 5) else solid
            moved = jnp.where(keep, stress[comp, x] + TIME_STEP * (rate - new), 0.0)
            write(comp, x, moved, new)


def stress_edge_kernel(core, first, table, velocity, stress, memory, *refs):
    cells, (pair, spread, outer, out, kept, own, given, rows, edges) = refs[:5], refs[5:]
    nx = stress.shape[1]
    place = edge_planes(nx)
    faces = Faces(VELOCITY, velocity, list(place), core[0], pair, spread, outer, rows, edges)
    faces.prepare()

    def write(comp, x, moved, new):
        out[comp, place[x]] = moved
        kept[comp, place[x]] = new

    stress_planes(faces, first, table, stress, memory, cells, write)
    pack_x(STRESS, out, place, nx, core[0], own, given)


def stress_rest_kernel(core, first, table, velocity, stress, memory, *refs):
    cells, (pair, spread, outer) = refs[:5], refs[5:8]
    edge, edge_kept, behind, out, kept, own, given, rows, edges = refs[8:]
    nx = stress.shape[1]
    place = edge_planes(nx)
    for x, at in place.items():
        for comp in range(6):
            out[comp, x] = edge[comp, at]
            kept[comp, x] = edge_kept[comp, at]
    inner = [x for x in range(nx) if x not in place]
    faces = Faces(VELOCITY, velocity, inner, core[0], pair, spread, outer, rows, edges)
    faces.prepare()

    def write(comp, x, moved, new):
        out[comp, x] = moved
        kept[comp, x] = new

    stress_planes(faces, first, table, stress, memory, cells, write)
    pack_yz(STRESS, out, core[0], own, given)


def last_kernel(core, first, table, velocity, stress, memory, *refs):
    cells, (pair, spread, outer, out, kept, rows, edges) = refs[:5], refs[5:]
    planes = list(range(stress.shape[1]))
    faces = Faces(VELOCITY, velocity, planes, core[0], pair, spread, outer, rows, edges)
    faces.prepare()

    def write(comp, x, moved, new):
        out[comp, x] = moved
        kept[comp, x] = new

    stress_planes(faces, first, table, stress, memory, cells, write)


def call(body, outs, operands, scalars=1, scratch=(), hold=False, cost=None):
    vmem = pl.BlockSpec(memory_space=pltpu.VMEM)
    specs = [pl.BlockSpec(memory_space=pltpu.SMEM)] * scalars
    specs += [vmem] * (len(operands) - scalars)
    if hold:
        specs[-1] = pl.BlockSpec(memory_space=pl.ANY)
    return pl.pallas_call(
        body,
        out_shape=outs,
        in_specs=specs,
        out_specs=[vmem] * len(outs),
        scratch_shapes=list(scratch),
        cost_estimate=cost,
        compiler_params=pltpu.CompilerParams(vmem_limit_bytes=24 * 1024 * 1024),
    )(*operands)


def float32(*shape):
    return jax.ShapeDtypeStruct(shape, jnp.float32)


def core_pairs(gy):
    return [[j, j + 1] for j in range(0, gy, 2)]


def send_x(core, own, given):
    gx, gy = lax.axis_size("gx"), lax.axis_size("gy")
    pair = lax.all_gather(given, "gy", axis=0, tiled=True, axis_index_groups=core_pairs(gy))
    (along,) = call(gather_x_kernel, [float32(2 * FACE, *own.shape[1:])], [core, own, pair])
    pairs = []
    for j in range(gy):
        step = 1 - 2 * (j % 2)
        pairs += [(i * gy + j, (i + step) * gy + j) for i in range(gx) if 0 <= i + step < gx]
    return along, lax.ppermute(along, ("gx", "gy"), pairs)


def send_yz(core, own, given, got_x):
    gy, gz = lax.axis_size("gy"), lax.axis_size("gz")
    plane = own.shape[1:]
    pair = lax.all_gather(given, "gy", axis=0, tiled=True, axis_index_groups=core_pairs(gy))
    along_y, along_z = call(
        gather_yz_kernel, [float32(FACE, *plane), float32(2, *plane)], [core, own, pair]
    )
    pairs = []
    for j in range(gy):
        step = 1 - 2 * (j % 2)
        pairs += [(j * gz + k, j * gz + k + step) for k in range(gz) if 0 <= k + step < gz]
    got_z = lax.ppermute(along_z, ("gy", "gz"), pairs)
    chips = [(j, j + 1) for j in range(1, gy - 1, 2)]
    outer = lax.ppermute(along_y, "gy", chips + [(k, j) for j, k in chips])
    (taken,) = call(join_kernel, [float32(TAKEN, *plane)], [got_x, got_z], scalars=0)
    spread = lax.all_gather(taken, "gy", axis=0, tiled=True, axis_index_groups=core_pairs(gy))
    return pair, spread, outer


def shards(
    velocity,
    stress,
    memory,
    lame_lambda,
    shear_modulus,
    buoyancy,
    anelastic_weight,
    decay_table,
    mech_index,
    surface_depth,
):
    nx, ny, nz = lame_lambda.shape
    core = (lax.axis_index("gy") % 2).astype(jnp.int32).reshape(1)
    first = (lax.axis_index("gz") * nz).astype(jnp.int32).reshape(1)
    like = lambda a: float32(*a.shape)
    scratch = (
        pltpu.VMEM((3, nx, ny + 16, nz), jnp.float32),
        pltpu.VMEM((3, nx * ny, nz), jnp.float32),
    )
    cost = pl.CostEstimate(flops=2**22, bytes_accessed=2**22, transcendentals=0)
    face_x = [float32(FACE, ny, nz)] * 2
    face_yz = [float32(GIVEN, ny, nz)] * 2
    cells = [lame_lambda, shear_modulus, anelastic_weight, mech_index, surface_depth]
    along, got_x = send_x(core, *call(first_x_kernel, face_x, [core, stress]))
    own, given = call(first_yz_kernel, face_yz, [core, stress, along], hold=True, cost=cost)
    for step in range(STEPS):
        halos = send_yz(core, own, given, got_x)
        operands = [core, stress, velocity, buoyancy, *halos]
        edge, own, given = call(
            velocity_edge_kernel, [float32(3, 4, ny, nz)] + face_x, operands, scratch=scratch
        )
        along, got_x = send_x(core, own, given)
        velocity, own, given = call(
            velocity_rest_kernel,
            [like(velocity)] + face_yz,
            operands + [edge, along],
            scratch=scratch,
            hold=True,
            cost=cost,
        )
        halos = send_yz(core, own, given, got_x)
        operands = [core, first, decay_table, velocity, stress, memory, *cells, *halos]
        if step == STEPS - 1:
            stress, memory = call(
                last_kernel, [like(stress), like(memory)], operands, scalars=3, scratch=scratch
            )
            break
        edge, edge_kept, own, given = call(
            stress_edge_kernel,
            [float32(6, 4, ny, nz)] * 2 + face_x,
            operands,
            scalars=3,
            scratch=scratch,
        )
        along, got_x = send_x(core, own, given)
        stress, memory, own, given = call(
            stress_rest_kernel,
            [like(stress), like(memory)] + face_yz,
            operands + [edge, edge_kept, along],
            scalars=3,
            scratch=scratch,
            hold=True,
            cost=cost,
        )
    return (velocity, stress, memory)


def solution(mesh):
    fields = P(None, *AXES)
    cells = P(*AXES)
    return jax.shard_map(
        shards,
        mesh=mesh,
        in_specs=(fields,) * 3 + (cells,) * 4 + (P(), cells, P("gx", "gy")),
        out_specs=(fields,) * 3,
        check_vma=False,
    )
```

```python
import jax
import jax.numpy as jnp
from jax import lax
from jax.experimental import pallas as pl
from jax.experimental.pallas import tpu as pltpu
from jax.sharding import PartitionSpec as P

STEPS = 2
COEF_NEAR = 9.0 / 8.0
COEF_FAR = -1.0 / 24.0
TIME_STEP = 0.2
AXES = ("gx", "gy", "gz")

STRESS = (
    ((0, "f"), (3, "b"), (4, "b")),
    ((3, "b"), (1, "f"), (5, "b")),
    ((4, "b"), (5, "b"), (2, "f")),
)
VELOCITY = (
    ((0, "b"), (1, "f"), (2, "f")),
    ((1, "b"), (0, "f"), (2, "f")),
    ((2, "b"), (0, "f"), (1, "f")),
)
BEFORE = {"f": (-1,), "b": (-2, -1)}
AFTER = {"f": (0, 1), "b": (0,)}
TAPS = {
    "f": ((1, COEF_NEAR), (0, -COEF_NEAR), (2, COEF_FAR), (-1, -COEF_FAR)),
    "b": ((0, COEF_NEAR), (-1, -COEF_NEAR), (1, COEF_FAR), (-2, -COEF_FAR)),
}

FACE = 5
TAKEN = 3 * FACE
LANES = 8


def edge_planes(nx):
    return {0: 0, 1: 1, nx - 2: 2, nx - 1: 3}


def layers(spec, sides):
    return [(comp, off) for comp, kind in spec for off in sides[kind]]


def weighted(taps):
    a, b, c, d = taps
    return COEF_NEAR * (a - b) + COEF_FAR * (c - d)


class Faces:
    def __init__(self, spec, fields, planes, core, halos, rows):
        self.spec, self.fields, self.planes, self.core, self.rows = spec, fields, planes, core, rows
        self.spread, self.outer, low, high = halos
        self.nx, self.ny, self.nz = fields.shape[1:]
        self.before = [{k: i for i, k in enumerate(layers(s, BEFORE))} for s in spec]
        self.after = [{k: i for i, k in enumerate(layers(s, AFTER))} for s in spec]
        self.low, self.high = low[...], high[...]
        self.lane = lax.broadcasted_iota(jnp.int32, (1, self.nz), 1)
        self.prepare()

    def prepare(self):
        ny = self.ny
        for slot, (comp, kind) in enumerate(self.spec[1]):
            for x in self.planes:
                self.rows[slot, x, 8 : 8 + ny, :] = self.fields[comp, x]

        def beside(before, after):
            for slot, (comp, kind) in enumerate(self.spec[1]):
                for x in self.planes:
                    for off in BEFORE[kind]:
                        i = self.before[1][comp, off]
                        self.rows[slot, x, 8 + off : 9 + off, :] = before(i, x)
                    for off in AFTER[kind]:
                        i = self.after[1][comp, off]
                        self.rows[slot, x, 8 + ny + off : 9 + ny + off, :] = after(i, x)

        outer = lambda i, x: self.outer[i, x : x + 1, :]

        @pl.when(self.core == 0)
        def _():
            beside(outer, lambda i, x: self.spread[TAKEN + 2 * FACE + i, x : x + 1, :])

        @pl.when(self.core == 1)
        def _():
            beside(lambda i, x: self.spread[2 * FACE + i, x : x + 1, :], outer)

    def dx(self, comp, x):
        kind = dict(self.spec[0])[comp]

        def plane(at):
            if at < 0:
                return self.spread[self.core * FACE + self.before[0][comp, at]]
            if at >= self.nx:
                return self.spread[TAKEN + self.core * FACE + self.after[0][comp, at - self.nx]]
            return self.fields[comp, at]

        return weighted([plane(x + off) for off, _ in TAPS[kind]])

    def dy(self, comp, x):
        slot = [c for c, _ in self.spec[1]].index(comp)
        kind = self.spec[1][slot][1]
        return weighted(
            [self.rows[slot, x, 8 + off : 8 + off + self.ny, :] for off, _ in TAPS[kind]]
        )

    def dz(self, comp, x):
        slot = [c for c, _ in self.spec[2]].index(comp)
        kind = self.spec[2][slot][1]
        nz, here = self.nz, self.fields[comp, x]
        first, count = self.before[2][comp, BEFORE[kind][0]], len(BEFORE[kind])
        low = pltpu.roll(self.low, (nz - count - LANES * x - first) % nz, 1)
        shift = (-LANES * x - self.after[2][comp, 0]) % nz
        high = pltpu.roll(self.high, shift, 1) if shift else self.high
        taps = {0: here}
        for off, _ in TAPS[kind]:
            if off < 0:
                taps[off] = pltpu.roll(jnp.where(self.lane >= nz + off, low, here), -off, 1)
            elif off > 0:
                taps[off] = pltpu.roll(jnp.where(self.lane < off, high, here), nz - off, 1)
        return weighted([taps[off] for off, _ in TAPS[kind]])


def pack_x(spec, fields, place, nx, core, own, given):
    def write(up, down):
        for i, (comp, off) in enumerate(layers(spec[0], BEFORE)):
            up[i] = fields[comp, place[nx + off]]
        for i, (comp, off) in enumerate(layers(spec[0], AFTER)):
            down[i] = fields[comp, place[off]]

    @pl.when(core == 0)
    def _():
        write(own, given)

    @pl.when(core == 1)
    def _():
        write(given, own)


def pack_yz(spec, fields, core, up, down, inner, outer):
    nx, ny, nz = fields.shape[1:]
    lane = lax.broadcasted_iota(jnp.int32, (1, nz), 1)
    for ref, sides in ((up, BEFORE), (down, AFTER)):
        total = jnp.zeros((ny, nz), jnp.float32)
        place = {k: i for i, k in enumerate(layers(spec[2], sides))}
        for comp, kind in spec[2]:
            offs = sides[kind]
            for x in range(nx):
                start = LANES * x + place[comp, offs[0]]
                shift = (start - offs[0]) % nz
                here = fields[comp, x]
                moved = pltpu.roll(here, shift, 1) if shift else here
                total = jnp.where((lane >= start) & (lane < start + len(offs)), moved, total)
        ref[...] = total

    def write(inner_sides, outer_sides):
        for ref, sides in ((inner, inner_sides), (outer, outer_sides)):
            for i, (comp, off) in enumerate(layers(spec[1], sides)):
                ref[i] = fields[comp, :, ny + off if sides is BEFORE else off, :]

    @pl.when(core == 0)
    def _():
        write(BEFORE, AFTER)

    @pl.when(core == 1)
    def _():
        write(AFTER, BEFORE)


def first_x_kernel(core, stress, own, given):
    nx = stress.shape[1]
    pack_x(STRESS, stress, {x: x for x in range(nx)}, nx, core[0], own, given)


def first_yz_kernel(core, stress, behind, *faces):
    pack_yz(STRESS, stress, core[0], *faces)


def gather_x_kernel(core, own, pair, along_x):
    here = core[0]
    there = 1 - here
    along_x[pl.ds(here * FACE, FACE)] = own[...]
    along_x[pl.ds(there * FACE, FACE)] = pair[pl.ds(there * FACE, FACE)]


def join_kernel(got_x, inner, taken):
    taken[: 2 * FACE] = got_x[...]
    taken[2 * FACE :] = inner[...]


def velocity_planes(faces, velocity, buoyancy, write):
    for x in faces.planes:
        scale = TIME_STEP * buoyancy[x]
        write(0, x, velocity[0, x] + scale * (faces.dx(0, x) + faces.dy(3, x) + faces.dz(4, x)))
        write(1, x, velocity[1, x] + scale * (faces.dx(3, x) + faces.dy(1, x) + faces.dz(5, x)))
        write(2, x, velocity[2, x] + scale * (faces.dx(4, x) + faces.dy(5, x) + faces.dz(2, x)))


def velocity_edge_kernel(core, stress, velocity, buoyancy, *refs):
    halos, (out, own, given, rows) = refs[:4], refs[4:]
    nx = stress.shape[1]
    place = edge_planes(nx)
    faces = Faces(STRESS, stress, list(place), core[0], halos, rows)

    def write(comp, x, value):
        out[comp, place[x]] = value

    velocity_planes(faces, velocity, buoyancy, write)
    pack_x(VELOCITY, out, place, nx, core[0], own, given)


def velocity_rest_kernel(core, stress, velocity, buoyancy, *refs):
    halos, (edge, behind, out, *packed, rows) = refs[:4], refs[4:]
    nx = stress.shape[1]
    place = edge_planes(nx)
    for x, at in place.items():
        for comp in range(3):
            out[comp, x] = edge[comp, at]
    inner = [x for x in range(nx) if x not in place]
    faces = Faces(STRESS, stress, inner, core[0], halos, rows)

    def write(comp, x, value):
        out[comp, x] = value

    velocity_planes(faces, velocity, buoyancy, write)
    pack_yz(VELOCITY, out, core[0], *packed)


def stress_planes(faces, first, table, stress, memory, cells, write):
    lam, shear, weight, mech, top_ref = cells
    nx, ny, nz = lam.shape
    tops = top_ref[...].astype(jnp.float32).T
    depth = (first[0] + lax.broadcasted_iota(jnp.int32, (1, nz), 1)).astype(jnp.float32)
    for x in faces.planes:
        decay = jnp.zeros((ny, nz), jnp.float32)
        for level in range(table.shape[0]):
            decay = jnp.where(mech[x] == level, table[level], decay)
        gain = (1.0 - decay) * weight[x]
        top = tops[:, x : x + 1]
        solid = depth >= top
        below = depth > top
        xx, yy, zz = faces.dx(0, x), faces.dy(1, x), faces.dz(2, x)
        volume = lam[x] * (xx + yy + zz)
        double = 2.0 * shear[x]
        rates = (
            volume + double * xx,
            volume + double * yy,
            volume + double * zz,
            shear[x] * (faces.dy(0, x) + faces.dx(1, x)),
            shear[x] * (faces.dz(0, x) + faces.dx(2, x)),
            shear[x] * (faces.dz(1, x) + faces.dy(2, x)),
        )
        for comp, rate in enumerate(rates):
            new = decay * memory[comp, x] + gain * rate
            keep = below if comp in (2, 4, 5) else solid
            moved = jnp.where(keep, stress[comp, x] + TIME_STEP * (rate - new), 0.0)
            write(comp, x, moved, new)


def stress_edge_kernel(core, first, table, velocity, stress, memory, *refs):
    cells, halos, (out, kept, own, given, rows) = refs[:5], refs[5:9], refs[9:]
    nx = stress.shape[1]
    place = edge_planes(nx)
    faces = Faces(VELOCITY, velocity, list(place), core[0], halos, rows)

    def write(comp, x, moved, new):
        out[comp, place[x]] = moved
        kept[comp, place[x]] = new

    stress_planes(faces, first, table, stress, memory, cells, write)
    pack_x(STRESS, out, place, nx, core[0], own, given)


def stress_rest_kernel(core, first, table, velocity, stress, memory, *refs):
    cells, halos = refs[:5], refs[5:9]
    edge, edge_kept, behind, out, kept, *packed, rows = refs[9:]
    nx = stress.shape[1]
    place = edge_planes(nx)
    for x, at in place.items():
        for comp in range(6):
            out[comp, x] = edge[comp, at]
            kept[comp, x] = edge_kept[comp, at]
    inner = [x for x in range(nx) if x not in place]
    faces = Faces(VELOCITY, velocity, inner, core[0], halos, rows)

    def write(comp, x, moved, new):
        out[comp, x] = moved
        kept[comp, x] = new

    stress_planes(faces, first, table, stress, memory, cells, write)
    pack_yz(STRESS, out, core[0], *packed)


def last_kernel(core, first, table, velocity, stress, memory, *refs):
    cells, halos, (out, kept, rows) = refs[:5], refs[5:9], refs[9:]
    planes = list(range(stress.shape[1]))
    faces = Faces(VELOCITY, velocity, planes, core[0], halos, rows)

    def write(comp, x, moved, new):
        out[comp, x] = moved
        kept[comp, x] = new

    stress_planes(faces, first, table, stress, memory, cells, write)


def call(body, outs, operands, scalars=1, scratch=(), hold=False, cost=None):
    vmem = pl.BlockSpec(memory_space=pltpu.VMEM)
    specs = [pl.BlockSpec(memory_space=pltpu.SMEM)] * scalars
    specs += [vmem] * (len(operands) - scalars)
    if hold:
        specs[-1] = pl.BlockSpec(memory_space=pl.ANY)
    return pl.pallas_call(
        body,
        out_shape=outs,
        in_specs=specs,
        out_specs=[vmem] * len(outs),
        scratch_shapes=list(scratch),
        cost_estimate=cost,
        compiler_params=pltpu.CompilerParams(vmem_limit_bytes=24 * 1024 * 1024),
    )(*operands)


def float32(*shape):
    return jax.ShapeDtypeStruct(shape, jnp.float32)


def core_pairs(gy):
    return [[j, j + 1] for j in range(0, gy, 2)]


def send_x(core, own, given):
    gx, gy = lax.axis_size("gx"), lax.axis_size("gy")
    pair = lax.all_gather(given, "gy", axis=0, tiled=True, axis_index_groups=core_pairs(gy))
    (along,) = call(gather_x_kernel, [float32(2 * FACE, *own.shape[1:])], [core, own, pair])
    pairs = []
    for j in range(gy):
        step = 1 - 2 * (j % 2)
        pairs += [(i * gy + j, (i + step) * gy + j) for i in range(gx) if 0 <= i + step < gx]
    return along, lax.ppermute(along, ("gx", "gy"), pairs)


def send_yz(up, down, inner, outer, got_x):
    gy, gz = lax.axis_size("gy"), lax.axis_size("gz")
    plane = up.shape
    pairs = [(k, k + 1) for k in range(gz - 1)]
    low = lax.ppermute(up, "gz", pairs)
    high = lax.ppermute(down, "gz", [(k, j) for j, k in pairs])
    chips = [(j, j + 1) for j in range(1, gy - 1, 2)]
    outer = lax.ppermute(outer, "gy", chips + [(k, j) for j, k in chips])
    (taken,) = call(join_kernel, [float32(TAKEN, *plane)], [got_x, inner], scalars=0)
    spread = lax.all_gather(taken, "gy", axis=0, tiled=True, axis_index_groups=core_pairs(gy))
    return spread, outer, low, high


def shards(
    velocity,
    stress,
    memory,
    lame_lambda,
    shear_modulus,
    buoyancy,
    anelastic_weight,
    decay_table,
    mech_index,
    surface_depth,
):
    nx, ny, nz = lame_lambda.shape
    core = (lax.axis_index("gy") % 2).astype(jnp.int32).reshape(1)
    first = (lax.axis_index("gz") * nz).astype(jnp.int32).reshape(1)
    like = lambda a: float32(*a.shape)
    scratch = [pltpu.VMEM((3, nx, ny + 16, nz), jnp.float32)]
    cost = pl.CostEstimate(flops=2**22, bytes_accessed=2**22, transcendentals=0)
    face_x = [float32(FACE, ny, nz)] * 2
    face_yz = [float32(ny, nz)] * 2 + [float32(FACE, ny, nz)] * 2
    cells = [lame_lambda, shear_modulus, anelastic_weight, mech_index, surface_depth]
    along, got_x = send_x(core, *call(first_x_kernel, face_x, [core, stress]))
    packed = call(first_yz_kernel, face_yz, [core, stress, along], hold=True, cost=cost)
    for step in range(STEPS):
        halos = send_yz(*packed, got_x)
        operands = [core, stress, velocity, buoyancy, *halos]
        edge, own, given = call(
            velocity_edge_kernel, [float32(3, 4, ny, nz)] + face_x, operands, scratch=scratch
        )
        along, got_x = send_x(core, own, given)
        velocity, *packed = call(
            velocity_rest_kernel,
            [like(velocity)] + face_yz,
            operands + [edge, along],
            scratch=scratch,
            hold=True,
            cost=cost,
        )
        halos = send_yz(*packed, got_x)
        operands = [core, first, decay_table, velocity, stress, memory, *cells, *halos]
        if step == STEPS - 1:
            stress, memory = call(
                last_kernel, [like(stress), like(memory)], operands, scalars=3, scratch=scratch
            )
            break
        edge, edge_kept, own, given = call(
            stress_edge_kernel,
            [float32(6, 4, ny, nz)] * 2 + face_x,
            operands,
            scalars=3,
            scratch=scratch,
        )
        along, got_x = send_x(core, own, given)
        stress, memory, *packed = call(
            stress_rest_kernel,
            [like(stress), like(memory)] + face_yz,
            operands + [edge, edge_kept, along],
            scalars=3,
            scratch=scratch,
            hold=True,
            cost=cost,
        )
    return (velocity, stress, memory)


def solution(mesh):
    fields = P(None, *AXES)
    cells = P(*AXES)
    return jax.shard_map(
        shards,
        mesh=mesh,
        in_specs=(fields,) * 3 + (cells,) * 4 + (P(), cells, P("gx", "gy")),
        out_specs=(fields,) * 3,
        check_vma=False,
    )
```

```python
import functools

import jax
import jax.numpy as jnp
from jax import lax
from jax.experimental import pallas as pl
from jax.experimental.pallas import tpu as pltpu
from jax.sharding import PartitionSpec as P

STEPS = 2
COEF_NEAR = 9.0 / 8.0
COEF_FAR = -1.0 / 24.0
TIME_STEP = 0.2
AXES = ("gx", "gy", "gz")

STRESS = (
    ((0, "f"), (3, "b"), (4, "b")),
    ((3, "b"), (1, "f"), (5, "b")),
    ((4, "b"), (5, "b"), (2, "f")),
)
VELOCITY = (
    ((0, "b"), (1, "f"), (2, "f")),
    ((1, "b"), (0, "f"), (2, "f")),
    ((2, "b"), (0, "f"), (1, "f")),
)
BEFORE = {"f": (-1,), "b": (-2, -1)}
AFTER = {"f": (0, 1), "b": (0,)}
TAPS = {
    "f": ((1, COEF_NEAR), (0, -COEF_NEAR), (2, COEF_FAR), (-1, -COEF_FAR)),
    "b": ((0, COEF_NEAR), (-1, -COEF_NEAR), (1, COEF_FAR), (-2, -COEF_FAR)),
}

FACE = 5
INNER = FACE + 1
GIVEN = INNER + FACE
TAKEN = 2 * FACE + 2


def layers(spec, sides):
    return [(comp, off) for comp, kind in spec for off in sides[kind]]


def weighted(taps):
    a, b, c, d = taps
    return COEF_NEAR * (a - b) + COEF_FAR * (c - d)


def thirds(value):
    high = value.astype(jnp.bfloat16)
    rest = value - high.astype(jnp.float32)
    middle = rest.astype(jnp.bfloat16)
    return high, middle, (rest - middle.astype(jnp.float32)).astype(jnp.bfloat16)


class Faces:
    def __init__(self, spec, fields, core, pair, spread, outer, rows, edges):
        self.spec, self.fields, self.rows, self.edges = spec, fields, rows, edges
        self.core, self.pair, self.spread, self.outer = core, pair, spread, outer
        self.nx, self.ny, self.nz = fields.shape[1:]
        self.before = [{k: i for i, k in enumerate(layers(s, BEFORE))} for s in spec]
        self.after = [{k: i for i, k in enumerate(layers(s, AFTER))} for s in spec]

    def prepare(self):
        nx, ny, nz = self.nx, self.ny, self.nz
        for slot, (comp, kind) in enumerate(self.spec[1]):
            for x in range(nx):
                self.rows[slot, x, 8 : 8 + ny, :] = self.fields[comp, x]

        def beside(before, after):
            for slot, (comp, kind) in enumerate(self.spec[1]):
                for x in range(nx):
                    for off in BEFORE[kind]:
                        i = self.before[1][comp, off]
                        self.rows[slot, x, 8 + off : 9 + off, :] = before(i, x)
                    for off in AFTER[kind]:
                        i = self.after[1][comp, off]
                        self.rows[slot, x, 8 + ny + off : 9 + ny + off, :] = after(i, x)

        outer = lambda i, x: self.outer[i, x : x + 1, :]

        @pl.when(self.core == 0)
        def _():
            beside(outer, lambda i, x: self.pair[GIVEN + INNER + i, x : x + 1, :])

        @pl.when(self.core == 1)
        def _():
            beside(lambda i, x: self.pair[INNER + i, x : x + 1, :], outer)

        ends = [self.spread[side * TAKEN + 2 * FACE + self.core] for side in (0, 1)]
        got = jnp.concatenate([jnp.concatenate([e[:8], e[8:]], axis=1) for e in ends], axis=0)
        row = lax.broadcasted_iota(jnp.int32, (16, nz), 0)
        lane = lax.broadcasted_iota(jnp.int32, (16, nz), 1)
        weights = []
        for comp, kind in self.spec[2]:
            here = jnp.zeros((16, nz), jnp.float32)
            for shift, weight in TAPS[kind]:
                scaled = float(round(24 * weight))
                for off in BEFORE[kind]:
                    at = off - shift
                    if 0 <= at < nz:
                        hit = (row == self.before[2][comp, off]) & (lane == at)
                        here = jnp.where(hit, scaled, here)
                for off in AFTER[kind]:
                    at = nz + off - shift
                    if 0 <= at < nz:
                        hit = (row == 8 + self.after[2][comp, off]) & (lane == at)
                        here = jnp.where(hit, scaled, here)
            weights.append(here)
        weights = jnp.concatenate(weights, axis=1).astype(jnp.bfloat16)
        weights = jnp.concatenate([weights] * 3, axis=0)
        stacked = jnp.concatenate([p.astype(jnp.float32) for p in thirds(got)], axis=0).T
        total = jnp.dot(stacked.astype(jnp.bfloat16), weights, preferred_element_type=jnp.float32)
        for slot in range(3):
            self.edges[slot] = total[:, slot * nz : (slot + 1) * nz] * (1.0 / 24.0)

    def dx(self, comp, x):
        kind = dict(self.spec[0])[comp]

        def plane(at):
            if at < 0:
                return self.spread[self.core * FACE + self.before[0][comp, at]]
            if at >= self.nx:
                return self.spread[TAKEN + self.core * FACE + self.after[0][comp, at - self.nx]]
            return self.fields[comp, at]

        return weighted([plane(x + off) for off, _ in TAPS[kind]])

    def dy(self, comp, x):
        slot = [c for c, _ in self.spec[1]].index(comp)
        kind = self.spec[1][slot][1]
        return weighted(
            [self.rows[slot, x, 8 + off : 8 + off + self.ny, :] for off, _ in TAPS[kind]]
        )

    def dz(self, comp, x):
        slot = [c for c, _ in self.spec[2]].index(comp)
        kind = self.spec[2][slot][1]
        here = self.fields[comp, x]
        lane = lax.broadcasted_iota(jnp.int32, (1, self.nz), 1)
        total = self.edges[slot, x * self.ny : (x + 1) * self.ny, :]
        for off, weight in TAPS[kind]:
            if off == 0:
                total = total + weight * here
            else:
                inside = (lane + off >= 0) & (lane + off < self.nz)
                moved = pltpu.roll(here, (-off) % self.nz, 1)
                total = total + jnp.where(inside, weight, 0.0) * moved
        return total


def pack(spec, fields, core, own, given):
    nx, ny, nz = fields.shape[1:]
    row = lax.broadcasted_iota(jnp.int32, (16, nz), 0)
    lane = lax.broadcasted_iota(jnp.int32, (16, nz), 1)
    before, after = layers(spec[2], BEFORE), layers(spec[2], AFTER)
    total = None
    for comp, _ in spec[2]:
        pick = jnp.zeros((16, nz), jnp.float32)
        for i, (c, off) in enumerate(before):
            if c == comp:
                pick = jnp.where((row == i) & (lane == nz + off), 1.0, pick)
        for i, (c, off) in enumerate(after):
            if c == comp:
                pick = jnp.where((row == 8 + i) & (lane == off), 1.0, pick)
        pick = pick.astype(jnp.bfloat16)
        for third in thirds(fields[comp].reshape(nx * ny, nz)):
            part = lax.dot_general(
                pick, third, (((1,), (1,)), ((), ())), preferred_element_type=jnp.float32
            )
            total = part if total is None else total + part
    half = nx * ny // 2
    ends = [jnp.concatenate([t[:, :half], t[:, half:]], axis=0) for t in (total[:8], total[8:])]

    def write(up, down, inner_up):
        for ref, sides in ((up, BEFORE), (down, AFTER)):
            for i, (comp, off) in enumerate(layers(spec[0], sides)):
                ref[i] = fields[comp, nx + off if sides is BEFORE else off]
        up[FACE] = ends[0]
        down[FACE] = ends[1]
        inner, outer = (BEFORE, AFTER) if inner_up else (AFTER, BEFORE)
        for ref, sides in ((given, inner), (own, outer)):
            for i, (comp, off) in enumerate(layers(spec[1], sides)):
                ref[INNER + i] = fields[comp, :, ny + off if sides is BEFORE else off, :]

    @pl.when(core == 0)
    def _():
        write(own, given, True)

    @pl.when(core == 1)
    def _():
        write(given, own, False)


def first_kernel(core, stress, own, given):
    pack(STRESS, stress, core[0], own, given)


def gather_kernel(core, own, pair, along_x, along_y, along_z):
    here = core[0]
    there = 1 - here
    other = there * GIVEN
    along_x[pl.ds(here * FACE, FACE)] = own[:FACE]
    along_x[pl.ds(there * FACE, FACE)] = pair[pl.ds(other, FACE)]
    along_z[here] = own[FACE]
    along_z[there] = pair[other + FACE]
    along_y[...] = own[INNER:]


def join_kernel(along_x, along_z, taken):
    taken[: 2 * FACE] = along_x[...]
    taken[2 * FACE :] = along_z[...]


def velocity_kernel(*refs):
    core, stress, velocity, buoyancy, pair, spread, outer, out = refs[:8]
    faces = Faces(STRESS, stress, core[0], pair, spread, outer, refs[-2], refs[-1])
    faces.prepare()
    for x in range(velocity.shape[1]):
        scale = TIME_STEP * buoyancy[x]
        out[0, x] = velocity[0, x] + scale * (faces.dx(0, x) + faces.dy(3, x) + faces.dz(4, x))
        out[1, x] = velocity[1, x] + scale * (faces.dx(3, x) + faces.dy(1, x) + faces.dz(5, x))
        out[2, x] = velocity[2, x] + scale * (faces.dx(4, x) + faces.dy(5, x) + faces.dz(2, x))
    pack(VELOCITY, out, core[0], *refs[8:10])


GROUPS = 4


def stress_kernel(send, *refs):
    core, first, table, velocity, stress, memory, lam, shear, weight, mech, top_ref = refs[:11]
    pair, spread, outer, out, kept = refs[11:16]
    if not send:
        finals = out, kept
        out, kept, sems = refs[16:19]
    faces = Faces(VELOCITY, velocity, core[0], pair, spread, outer, refs[-2], refs[-1])
    faces.prepare()
    nx, ny, nz = lam.shape
    tops = top_ref[...].astype(jnp.float32).T
    depth = (first[0] + lax.broadcasted_iota(jnp.int32, (1, nz), 1)).astype(jnp.float32)
    copies = []
    for x in range(nx):
        decay = jnp.zeros((ny, nz), jnp.float32)
        for level in range(table.shape[0]):
            decay = jnp.where(mech[x] == level, table[level], decay)
        gain = (1.0 - decay) * weight[x]
        top = tops[:, x : x + 1]
        solid = depth >= top
        below = depth > top
        xx, yy, zz = faces.dx(0, x), faces.dy(1, x), faces.dz(2, x)
        volume = lam[x] * (xx + yy + zz)
        double = 2.0 * shear[x]
        rates = (
            volume + double * xx,
            volume + double * yy,
            volume + double * zz,
            shear[x] * (faces.dy(0, x) + faces.dx(1, x)),
            shear[x] * (faces.dz(0, x) + faces.dx(2, x)),
            shear[x] * (faces.dz(1, x) + faces.dy(2, x)),
        )
        for comp, rate in enumerate(rates):
            new = decay * memory[comp, x] + gain * rate
            kept[comp, x] = new
            keep = below if comp in (2, 4, 5) else solid
            out[comp, x] = jnp.where(keep, stress[comp, x] + TIME_STEP * (rate - new), 0.0)
        size = nx // GROUPS
        if not send and (x + 1) % size == 0:
            part = pl.ds(x + 1 - size, size)
            for i, (held, final) in enumerate(zip((out, kept), finals)):
                copy = pltpu.make_async_copy(
                    held.at[:, part], final.at[:, part], sems.at[i, x // size]
                )
                copy.start()
                copies.append(copy)
    for copy in copies:
        copy.wait()
    if send:
        pack(STRESS, out, core[0], *refs[16:18])


def call(body, outs, operands, scalars=1, scratch=(), out_space=pltpu.VMEM):
    vmem = pl.BlockSpec(memory_space=pltpu.VMEM)
    smem = pl.BlockSpec(memory_space=pltpu.SMEM)
    return pl.pallas_call(
        body,
        out_shape=outs,
        in_specs=[smem if i < scalars else vmem for i in range(len(operands))],
        out_specs=[pl.BlockSpec(memory_space=out_space)] * len(outs),
        scratch_shapes=list(scratch),
        compiler_params=pltpu.CompilerParams(vmem_limit_bytes=24 * 1024 * 1024),
    )(*operands)


def exchange(core, own, given):
    plane = own.shape[1:]
    planes = lambda n: jax.ShapeDtypeStruct((n,) + plane, own.dtype)
    gx, gy, gz = [lax.axis_size(axis) for axis in AXES]
    cores = [[j, j + 1] for j in range(0, gy, 2)]
    pair = lax.all_gather(given, "gy", axis=0, tiled=True, axis_index_groups=cores)
    along_x, along_y, along_z = call(
        gather_kernel, [planes(2 * FACE), planes(FACE), planes(2)], [core, own, pair]
    )
    to_x, to_z = [], []
    for j in range(gy):
        step = 1 - 2 * (j % 2)
        to_x += [(i * gy + j, (i + step) * gy + j) for i in range(gx) if 0 <= i + step < gx]
        to_z += [(j * gz + k, j * gz + k + step) for k in range(gz) if 0 <= k + step < gz]
    to_y = [(j, j + 1) for j in range(1, gy - 1, 2)] + [(j + 1, j) for j in range(1, gy - 1, 2)]
    got_x = lax.ppermute(along_x, ("gx", "gy"), to_x)
    got_z = lax.ppermute(along_z, ("gy", "gz"), to_z)
    outer = lax.ppermute(along_y, "gy", to_y)
    (taken,) = call(join_kernel, [planes(TAKEN)], [got_x, got_z], scalars=0)
    spread = lax.all_gather(taken, "gy", axis=0, tiled=True, axis_index_groups=cores)
    return pair, spread, outer


def shards(
    velocity,
    stress,
    memory,
    lame_lambda,
    shear_modulus,
    buoyancy,
    anelastic_weight,
    decay_table,
    mech_index,
    surface_depth,
):
    nx, ny, nz = lame_lambda.shape
    core = (lax.axis_index("gy") % 2).astype(jnp.int32).reshape(1)
    first = (lax.axis_index("gz") * nz).astype(jnp.int32).reshape(1)
    like = lambda a: jax.ShapeDtypeStruct(a.shape, a.dtype)
    packed = [jax.ShapeDtypeStruct((GIVEN, ny, nz), jnp.float32)] * 2
    scratch = (
        pltpu.VMEM((3, nx, ny + 16, nz), jnp.float32),
        pltpu.VMEM((3, nx * ny, nz), jnp.float32),
    )
    held = (
        pltpu.VMEM(stress.shape, jnp.float32),
        pltpu.VMEM(memory.shape, jnp.float32),
        pltpu.SemaphoreType.DMA((2, GROUPS)),
    )
    own, given = call(first_kernel, packed, [core, stress])
    for step in range(STEPS):
        velocity, own, given = call(
            velocity_kernel,
            [like(velocity)] + packed,
            [core, stress, velocity, buoyancy, *exchange(core, own, given)],
            scratch=scratch,
        )
        send = step < STEPS - 1
        stress, memory, *rest = call(
            functools.partial(stress_kernel, send),
            [like(stress), like(memory)] + (packed if send else []),
            [
                core,
                first,
                decay_table,
                velocity,
                stress,
                memory,
                lame_lambda,
                shear_modulus,
                anelastic_weight,
                mech_index,
                surface_depth,
                *exchange(core, own, given),
            ],
            scalars=3,
            scratch=scratch if send else held + scratch,
            out_space=pltpu.VMEM if send else pl.ANY,
        )
        if send:
            own, given = rest
    return (velocity, stress, memory)


def solution(mesh):
    fields = P(None, *AXES)
    cells = P(*AXES)
    return jax.shard_map(
        shards,
        mesh=mesh,
        in_specs=(fields,) * 3 + (cells,) * 4 + (P(), cells, P("gx", "gy")),
        out_specs=(fields,) * 3,
        check_vma=False,
    )
```

```python
import functools

import jax
import jax.numpy as jnp
from jax import lax
from jax.experimental import pallas as pl
from jax.experimental.pallas import tpu as pltpu
from jax.sharding import PartitionSpec as P

STEPS = 2
COEF_NEAR = 9.0 / 8.0
COEF_FAR = -1.0 / 24.0
TIME_STEP = 0.2
AXES = ("gx", "gy", "gz")

STRESS = (
    ((0, "f"), (3, "b"), (4, "b")),
    ((3, "b"), (1, "f"), (5, "b")),
    ((4, "b"), (5, "b"), (2, "f")),
)
VELOCITY = (
    ((0, "b"), (1, "f"), (2, "f")),
    ((1, "b"), (0, "f"), (2, "f")),
    ((2, "b"), (0, "f"), (1, "f")),
)
BEFORE = {"f": (-1,), "b": (-2, -1)}
AFTER = {"f": (0, 1), "b": (0,)}
TAPS = {
    "f": ((1, COEF_NEAR), (0, -COEF_NEAR), (2, COEF_FAR), (-1, -COEF_FAR)),
    "b": ((0, COEF_NEAR), (-1, -COEF_NEAR), (1, COEF_FAR), (-2, -COEF_FAR)),
}

GROUPS = 4
FACE = 5
INNER = FACE + 1
GIVEN = INNER + FACE
TAKEN = 2 * FACE + 2


def layers(spec, sides):
    return [(comp, off) for comp, kind in spec for off in sides[kind]]


def weighted(taps):
    a, b, c, d = taps
    return COEF_NEAR * (a - b) + COEF_FAR * (c - d)


def thirds(value):
    high = value.astype(jnp.bfloat16)
    rest = value - high.astype(jnp.float32)
    middle = rest.astype(jnp.bfloat16)
    return high, middle, (rest - middle.astype(jnp.float32)).astype(jnp.bfloat16)


class Near:
    def __init__(self, spec, fields, core, pair, outer, rows):
        self.spec, self.fields, self.rows = spec, fields, rows
        self.nx, self.ny, self.nz = nx, ny, nz = fields.shape[1:]
        first = {k: i for i, k in enumerate(layers(spec[1], BEFORE))}
        last = {k: i for i, k in enumerate(layers(spec[1], AFTER))}
        for slot, (comp, kind) in enumerate(spec[1]):
            for x in range(nx):
                rows[slot, x, 8 : 8 + ny, :] = fields[comp, x]

        def beside(before, after):
            for slot, (comp, kind) in enumerate(spec[1]):
                for x in range(nx):
                    for off in BEFORE[kind]:
                        rows[slot, x, 8 + off : 9 + off, :] = before(first[comp, off], x)
                    for off in AFTER[kind]:
                        rows[slot, x, 8 + ny + off : 9 + ny + off, :] = after(last[comp, off], x)

        beyond = lambda i, x: outer[i, x : x + 1, :]

        @pl.when(core == 0)
        def _():
            beside(beyond, lambda i, x: pair[GIVEN + INNER + i, x : x + 1, :])

        @pl.when(core == 1)
        def _():
            beside(lambda i, x: pair[INNER + i, x : x + 1, :], beyond)

    def dx(self, comp, x):
        taps = TAPS[dict(self.spec[0])[comp]]
        if all(0 <= x + off < self.nx for off, _ in taps):
            return weighted([self.fields[comp, x + off] for off, _ in taps])
        return sum(w * self.fields[comp, x + off] for off, w in taps if 0 <= x + off < self.nx)

    def dy(self, comp, x):
        slot = [c for c, _ in self.spec[1]].index(comp)
        kind = self.spec[1][slot][1]
        return weighted(
            [self.rows[slot, x, 8 + off : 8 + off + self.ny, :] for off, _ in TAPS[kind]]
        )

    def dz(self, comp, x):
        here = self.fields[comp, x]
        lane = lax.broadcasted_iota(jnp.int32, (1, self.nz), 1)
        total = None
        for off, weight in TAPS[dict(self.spec[2])[comp]]:
            if off == 0:
                term = weight * here
            else:
                inside = (lane + off >= 0) & (lane + off < self.nz)
                term = jnp.where(inside, weight, 0.0) * pltpu.roll(here, (-off) % self.nz, 1)
            total = term if total is None else total + term
        return total


class Far:
    def __init__(self, spec, shape, core, spread, edges):
        self.spec, self.core, self.spread, self.edges = spec, core, spread, edges
        self.nx, self.ny, self.nz = nx, ny, nz = shape
        self.before = [{k: i for i, k in enumerate(layers(s, BEFORE))} for s in spec]
        self.after = [{k: i for i, k in enumerate(layers(s, AFTER))} for s in spec]
        ends = [spread[side * TAKEN + 2 * FACE + core] for side in (0, 1)]
        got = jnp.concatenate([jnp.concatenate([e[:8], e[8:]], axis=1) for e in ends], axis=0)
        row = lax.broadcasted_iota(jnp.int32, (16, nz), 0)
        lane = lax.broadcasted_iota(jnp.int32, (16, nz), 1)
        weights = []
        for comp, kind in spec[2]:
            here = jnp.zeros((16, nz), jnp.float32)
            for shift, weight in TAPS[kind]:
                scaled = float(round(24 * weight))
                places = [(self.before[2][comp, off], off - shift) for off in BEFORE[kind]]
                places += [(8 + self.after[2][comp, off], nz + off - shift) for off in AFTER[kind]]
                for i, at in places:
                    if 0 <= at < nz:
                        here = jnp.where((row == i) & (lane == at), scaled, here)
            weights.append(here)
        weights = jnp.concatenate(weights, axis=1).astype(jnp.bfloat16)
        weights = jnp.concatenate([weights] * 3, axis=0)
        stacked = jnp.concatenate([p.astype(jnp.float32) for p in thirds(got)], axis=0).T
        total = jnp.dot(stacked.astype(jnp.bfloat16), weights, preferred_element_type=jnp.float32)
        for slot in range(3):
            edges[slot] = total[:, slot * nz : (slot + 1) * nz] * (1.0 / 24.0)

    def dx(self, comp, x):
        total = 0.0
        for off, weight in TAPS[dict(self.spec[0])[comp]]:
            at = x + off
            if at < 0:
                here = self.spread[self.core * FACE + self.before[0][comp, at]]
                total = total + weight * here
            elif at >= self.nx:
                i = self.after[0][comp, at - self.nx]
                total = total + weight * self.spread[TAKEN + self.core * FACE + i]
        return total

    def dz(self, comp, x):
        slot = [c for c, _ in self.spec[2]].index(comp)
        return self.edges[slot, x * self.ny : (x + 1) * self.ny, :]


def pack(spec, fields, core, own, given):
    nx, ny, nz = fields.shape[1:]
    row = lax.broadcasted_iota(jnp.int32, (16, nz), 0)
    lane = lax.broadcasted_iota(jnp.int32, (16, nz), 1)
    before, after = layers(spec[2], BEFORE), layers(spec[2], AFTER)
    total = None
    for comp, _ in spec[2]:
        pick = jnp.zeros((16, nz), jnp.float32)
        for i, (c, off) in enumerate(before):
            if c == comp:
                pick = jnp.where((row == i) & (lane == nz + off), 1.0, pick)
        for i, (c, off) in enumerate(after):
            if c == comp:
                pick = jnp.where((row == 8 + i) & (lane == off), 1.0, pick)
        pick = pick.astype(jnp.bfloat16)
        for third in thirds(fields[comp].reshape(nx * ny, nz)):
            part = lax.dot_general(
                pick, third, (((1,), (1,)), ((), ())), preferred_element_type=jnp.float32
            )
            total = part if total is None else total + part
    half = nx * ny // 2
    ends = [jnp.concatenate([t[:, :half], t[:, half:]], axis=0) for t in (total[:8], total[8:])]

    def write(up, down, inner_up):
        for ref, sides in ((up, BEFORE), (down, AFTER)):
            for i, (comp, off) in enumerate(layers(spec[0], sides)):
                ref[i] = fields[comp, nx + off if sides is BEFORE else off]
        up[FACE] = ends[0]
        down[FACE] = ends[1]
        inner, outer = (BEFORE, AFTER) if inner_up else (AFTER, BEFORE)
        for ref, sides in ((given, inner), (own, outer)):
            for i, (comp, off) in enumerate(layers(spec[1], sides)):
                ref[INNER + i] = fields[comp, :, ny + off if sides is BEFORE else off, :]

    @pl.when(core == 0)
    def _():
        write(own, given, True)

    @pl.when(core == 1)
    def _():
        write(given, own, False)


def first_kernel(core, stress, own, given):
    pack(STRESS, stress, core[0], own, given)


def gather_kernel(core, own, pair, along_x, along_y, along_z):
    here = core[0]
    there = 1 - here
    other = there * GIVEN
    along_x[pl.ds(here * FACE, FACE)] = own[:FACE]
    along_x[pl.ds(there * FACE, FACE)] = pair[pl.ds(other, FACE)]
    along_z[here] = own[FACE]
    along_z[there] = pair[other + FACE]
    along_y[...] = own[INNER:]


def join_kernel(along_x, along_z, near, taken):
    taken[: 2 * FACE] = along_x[...]
    taken[2 * FACE :] = along_z[...]


def cells_kernel(first, table, mech, weight, top, behind, decay, gain, limits):
    limits[...] = (top[...] - first[0]).astype(jnp.float32).T
    for x in range(mech.shape[0]):
        here = jnp.zeros(mech.shape[1:], jnp.float32)
        for level in range(table.shape[0]):
            here = jnp.where(mech[x] == level, table[level], here)
        decay[x] = here
        gain[x] = (1.0 - here) * weight[x]


def near_velocity_kernel(core, stress, velocity, buoyancy, pair, outer, behind, out, rows):
    near = Near(STRESS, stress, core[0], pair, outer, rows)
    for x in range(velocity.shape[1]):
        scale = TIME_STEP * buoyancy[x]
        out[0, x] = velocity[0, x] + scale * (near.dx(0, x) + near.dy(3, x) + near.dz(4, x))
        out[1, x] = velocity[1, x] + scale * (near.dx(3, x) + near.dy(1, x) + near.dz(5, x))
        out[2, x] = velocity[2, x] + scale * (near.dx(4, x) + near.dy(5, x) + near.dz(2, x))


def velocity_kernel(core, near, buoyancy, spread, out, own, given, edges):
    far = Far(STRESS, near.shape[1:], core[0], spread, edges)
    for x in range(near.shape[1]):
        scale = TIME_STEP * buoyancy[x]
        out[0, x] = near[0, x] + scale * (far.dx(0, x) + far.dz(4, x))
        out[1, x] = near[1, x] + scale * (far.dx(3, x) + far.dz(5, x))
        out[2, x] = near[2, x] + scale * (far.dx(4, x) + far.dz(2, x))
    pack(VELOCITY, out, core[0], own, given)


def near_strain_kernel(core, velocity, pair, outer, behind, out, rows):
    near = Near(VELOCITY, velocity, core[0], pair, outer, rows)
    for x in range(velocity.shape[1]):
        out[0, x] = near.dx(0, x)
        out[1, x] = near.dy(1, x)
        out[2, x] = near.dz(2, x)
        out[3, x] = near.dy(0, x) + near.dx(1, x)
        out[4, x] = near.dz(0, x) + near.dx(2, x)
        out[5, x] = near.dz(1, x) + near.dy(2, x)


def stress_kernel(send, core, near, stress, memory, lam, shear, decay, gain, limits, *refs):
    if send:
        spread, out, kept, own, given, edges = refs
    else:
        spread, *finals, out, kept, sems, edges = refs
    nx, ny, nz = lam.shape
    far = Far(VELOCITY, lam.shape, core[0], spread, edges)
    depth = lax.broadcasted_iota(jnp.int32, (1, nz), 1).astype(jnp.float32)
    copies = []
    for x in range(nx):
        top = limits[:, x : x + 1]
        solid = depth >= top
        below = depth > top
        xx, yy, zz = near[0, x] + far.dx(0, x), near[1, x], near[2, x] + far.dz(2, x)
        volume = lam[x] * (xx + yy + zz)
        double = 2.0 * shear[x]
        rates = (
            volume + double * xx,
            volume + double * yy,
            volume + double * zz,
            shear[x] * (near[3, x] + far.dx(1, x)),
            shear[x] * (near[4, x] + far.dz(0, x) + far.dx(2, x)),
            shear[x] * (near[5, x] + far.dz(1, x)),
        )
        for comp, rate in enumerate(rates):
            new = decay[x] * memory[comp, x] + gain[x] * rate
            kept[comp, x] = new
            keep = below if comp in (2, 4, 5) else solid
            out[comp, x] = jnp.where(keep, stress[comp, x] + TIME_STEP * (rate - new), 0.0)
        size = nx // GROUPS
        if not send and (x + 1) % size == 0:
            part = pl.ds(x + 1 - size, size)
            for i, (held, final) in enumerate(zip((out, kept), finals)):
                copy = pltpu.make_async_copy(
                    held.at[:, part], final.at[:, part], sems.at[i, x // size]
                )
                copy.start()
                copies.append(copy)
    for copy in copies:
        copy.wait()
    if send:
        pack(STRESS, out, core[0], own, given)


def call(body, outs, operands, scalars=1, scratch=(), hold=False, out_space=pltpu.VMEM):
    vmem = pl.BlockSpec(memory_space=pltpu.VMEM)
    specs = [pl.BlockSpec(memory_space=pltpu.SMEM)] * scalars
    specs += [vmem] * (len(operands) - scalars)
    if hold:
        specs[-1] = pl.BlockSpec(memory_space=pl.ANY)
    return pl.pallas_call(
        body,
        out_shape=outs,
        in_specs=specs,
        out_specs=[pl.BlockSpec(memory_space=out_space)] * len(outs),
        scratch_shapes=list(scratch),
        cost_estimate=pl.CostEstimate(flops=2**22, bytes_accessed=2**22, transcendentals=0)
        if hold
        else None,
        compiler_params=pltpu.CompilerParams(vmem_limit_bytes=24 * 1024 * 1024),
    )(*operands)


def exchange(core, own, given, near_kernel):
    plane = own.shape[1:]
    planes = lambda n: jax.ShapeDtypeStruct((n,) + plane, own.dtype)
    gx, gy, gz = [lax.axis_size(axis) for axis in AXES]
    cores = [[j, j + 1] for j in range(0, gy, 2)]
    pair = lax.all_gather(given, "gy", axis=0, tiled=True, axis_index_groups=cores)
    along_x, along_y, along_z = call(
        gather_kernel, [planes(2 * FACE), planes(FACE), planes(2)], [core, own, pair]
    )
    to_x, to_z = [], []
    for j in range(gy):
        step = 1 - 2 * (j % 2)
        to_x += [(i * gy + j, (i + step) * gy + j) for i in range(gx) if 0 <= i + step < gx]
        to_z += [(j * gz + k, j * gz + k + step) for k in range(gz) if 0 <= k + step < gz]
    to_y = [(j, j + 1) for j in range(1, gy - 1, 2)] + [(j + 1, j) for j in range(1, gy - 1, 2)]
    got_x = lax.ppermute(along_x, ("gx", "gy"), to_x)
    got_z = lax.ppermute(along_z, ("gy", "gz"), to_z)
    outer = lax.ppermute(along_y, "gy", to_y)
    near = near_kernel(pair, outer, along_x)
    (taken,) = call(join_kernel, [planes(TAKEN)], [got_x, got_z, near], scalars=0, hold=True)
    spread = lax.all_gather(taken, "gy", axis=0, tiled=True, axis_index_groups=cores)
    return near, spread, along_x


def shards(
    velocity,
    stress,
    memory,
    lame_lambda,
    shear_modulus,
    buoyancy,
    anelastic_weight,
    decay_table,
    mech_index,
    surface_depth,
):
    nx, ny, nz = lame_lambda.shape
    core = (lax.axis_index("gy") % 2).astype(jnp.int32).reshape(1)
    first = (lax.axis_index("gz") * nz).astype(jnp.int32).reshape(1)
    like = lambda a: jax.ShapeDtypeStruct(a.shape, jnp.float32)
    packed = [jax.ShapeDtypeStruct((GIVEN, ny, nz), jnp.float32)] * 2
    rows = [pltpu.VMEM((3, nx, ny + 16, nz), jnp.float32)]
    edges = [pltpu.VMEM((3, nx * ny, nz), jnp.float32)]
    held = [
        pltpu.VMEM(stress.shape, jnp.float32),
        pltpu.VMEM(memory.shape, jnp.float32),
        pltpu.SemaphoreType.DMA((2, GROUPS)),
    ]
    own, given = call(first_kernel, packed, [core, stress])
    for step in range(STEPS):

        def near_velocity(*got):
            operands = [core, stress, velocity, buoyancy, *got]
            outs = [like(velocity)]
            return call(near_velocity_kernel, outs, operands, scratch=rows, hold=True)[0]

        def near_strain(*got):
            outs = [like(stress)]
            return call(near_strain_kernel, outs, [core, velocity, *got], scratch=rows, hold=True)[0]

        near, spread, along = exchange(core, own, given, near_velocity)
        if step == 0:
            cells = call(
                cells_kernel,
                [like(lame_lambda)] * 2 + [like(surface_depth)],
                [first, decay_table, mech_index, anelastic_weight, surface_depth, along],
                scalars=2,
                hold=True,
            )
        velocity, own, given = call(
            velocity_kernel,
            [like(velocity)] + packed,
            [core, near, buoyancy, spread],
            scratch=edges,
        )
        near, spread, _ = exchange(core, own, given, near_strain)
        send = step < STEPS - 1
        stress, memory, *rest = call(
            functools.partial(stress_kernel, send),
            [like(stress), like(memory)] + (packed if send else []),
            [core, near, stress, memory, lame_lambda, shear_modulus, *cells, spread],
            scratch=edges if send else held + edges,
            out_space=pltpu.VMEM if send else pl.ANY,
        )
        if send:
            own, given = rest
    return (velocity, stress, memory)


def solution(mesh):
    fields = P(None, *AXES)
    cells = P(*AXES)
    return jax.shard_map(
        shards,
        mesh=mesh,
        in_specs=(fields,) * 3 + (cells,) * 4 + (P(), cells, P("gx", "gy")),
        out_specs=(fields,) * 3,
        check_vma=False,
    )
```

```python
import functools

import jax
import jax.numpy as jnp
from jax import lax
from jax.experimental import pallas as pl
from jax.experimental.pallas import tpu as pltpu
from jax.sharding import PartitionSpec as P

STEPS = 2
COEF_NEAR = 9.0 / 8.0
COEF_FAR = -1.0 / 24.0
TIME_STEP = 0.2
AXES = ("gx", "gy", "gz")

STRESS = (
    ((0, "f"), (3, "b"), (4, "b")),
    ((3, "b"), (1, "f"), (5, "b")),
    ((4, "b"), (5, "b"), (2, "f")),
)
VELOCITY = (
    ((0, "b"), (1, "f"), (2, "f")),
    ((1, "b"), (0, "f"), (2, "f")),
    ((2, "b"), (0, "f"), (1, "f")),
)
BEFORE = {"f": (-1,), "b": (-2, -1)}
AFTER = {"f": (0, 1), "b": (0,)}
TAPS = {
    "f": ((1, COEF_NEAR), (0, -COEF_NEAR), (2, COEF_FAR), (-1, -COEF_FAR)),
    "b": ((0, COEF_NEAR), (-1, -COEF_NEAR), (1, COEF_FAR), (-2, -COEF_FAR)),
}

GROUPS = 4
FACE = 5
INNER = FACE + 1
GIVEN = INNER + FACE
TAKEN = 2 * FACE + 2


def layers(spec, sides):
    return [(comp, off) for comp, kind in spec for off in sides[kind]]


def weighted(taps):
    a, b, c, d = taps
    return COEF_NEAR * (a - b) + COEF_FAR * (c - d)


def thirds(value):
    high = value.astype(jnp.bfloat16)
    rest = value - high.astype(jnp.float32)
    middle = rest.astype(jnp.bfloat16)
    return high, middle, (rest - middle.astype(jnp.float32)).astype(jnp.bfloat16)


class Near:
    def __init__(self, spec, fields, core, pair, rows):
        self.spec, self.fields, self.rows = spec, fields, rows
        self.nx, self.ny, self.nz = nx, ny, nz = fields.shape[1:]
        first = {k: i for i, k in enumerate(layers(spec[1], BEFORE))}
        last = {k: i for i, k in enumerate(layers(spec[1], AFTER))}
        for slot, (comp, kind) in enumerate(spec[1]):
            for x in range(nx):
                rows[slot, x, 8 : 8 + ny, :] = fields[comp, x]

        def beside(before, after):
            for slot, (comp, kind) in enumerate(spec[1]):
                for x in range(nx):
                    for off in BEFORE[kind]:
                        rows[slot, x, 8 + off : 9 + off, :] = before(first[comp, off], x)
                    for off in AFTER[kind]:
                        rows[slot, x, 8 + ny + off : 9 + ny + off, :] = after(last[comp, off], x)

        beyond = lambda i, x: jnp.zeros((1, nz), jnp.float32)

        @pl.when(core == 0)
        def _():
            beside(beyond, lambda i, x: pair[GIVEN + INNER + i, x : x + 1, :])

        @pl.when(core == 1)
        def _():
            beside(lambda i, x: pair[INNER + i, x : x + 1, :], beyond)

    def dx(self, comp, x):
        taps = TAPS[dict(self.spec[0])[comp]]
        if all(0 <= x + off < self.nx for off, _ in taps):
            return weighted([self.fields[comp, x + off] for off, _ in taps])
        return sum(w * self.fields[comp, x + off] for off, w in taps if 0 <= x + off < self.nx)

    def dy(self, comp, x):
        slot = [c for c, _ in self.spec[1]].index(comp)
        kind = self.spec[1][slot][1]
        return weighted(
            [self.rows[slot, x, 8 + off : 8 + off + self.ny, :] for off, _ in TAPS[kind]]
        )

    def dz(self, comp, x):
        here = self.fields[comp, x]
        lane = lax.broadcasted_iota(jnp.int32, (1, self.nz), 1)
        total = None
        for off, weight in TAPS[dict(self.spec[2])[comp]]:
            if off == 0:
                term = weight * here
            else:
                inside = (lane + off >= 0) & (lane + off < self.nz)
                term = jnp.where(inside, weight, 0.0) * pltpu.roll(here, (-off) % self.nz, 1)
            total = term if total is None else total + term
        return total


class Far:
    def __init__(self, spec, shape, core, spread, edges):
        self.spec, self.core, self.spread, self.edges = spec, core, spread, edges
        self.nx, self.ny, self.nz = nx, ny, nz = shape
        self.before = [{k: i for i, k in enumerate(layers(s, BEFORE))} for s in spec]
        self.after = [{k: i for i, k in enumerate(layers(s, AFTER))} for s in spec]
        ends = [spread[side * TAKEN + 2 * FACE + core] for side in (0, 1)]
        got = jnp.concatenate([jnp.concatenate([e[:8], e[8:]], axis=1) for e in ends], axis=0)
        row = lax.broadcasted_iota(jnp.int32, (16, nz), 0)
        lane = lax.broadcasted_iota(jnp.int32, (16, nz), 1)
        weights = []
        for comp, kind in spec[2]:
            here = jnp.zeros((16, nz), jnp.float32)
            for shift, weight in TAPS[kind]:
                scaled = float(round(24 * weight))
                places = [(self.before[2][comp, off], off - shift) for off in BEFORE[kind]]
                places += [(8 + self.after[2][comp, off], nz + off - shift) for off in AFTER[kind]]
                for i, at in places:
                    if 0 <= at < nz:
                        here = jnp.where((row == i) & (lane == at), scaled, here)
            weights.append(here)
        weights = jnp.concatenate(weights, axis=1).astype(jnp.bfloat16)
        weights = jnp.concatenate([weights] * 3, axis=0)
        stacked = jnp.concatenate([p.astype(jnp.float32) for p in thirds(got)], axis=0).T
        total = jnp.dot(stacked.astype(jnp.bfloat16), weights, preferred_element_type=jnp.float32)
        for slot in range(3):
            edges[slot] = total[:, slot * nz : (slot + 1) * nz] * (1.0 / 24.0)

    def dx(self, comp, x):
        total = 0.0
        for off, weight in TAPS[dict(self.spec[0])[comp]]:
            at = x + off
            if at < 0:
                here = self.spread[self.core * FACE + self.before[0][comp, at]]
                total = total + weight * here
            elif at >= self.nx:
                i = self.after[0][comp, at - self.nx]
                total = total + weight * self.spread[TAKEN + self.core * FACE + i]
        return total

    def outer_rows(self, outer, add):
        ny = self.ny

        def rows(sides, place, base):
            for slot, (comp, kind) in enumerate(self.spec[1]):
                terms = {}
                for off in sides[kind]:
                    for shift, weight in TAPS[kind]:
                        at = base + off - shift
                        if 0 <= at < ny:
                            term = weight * outer[place[comp, off]]
                            terms[at] = terms[at] + term if at in terms else term
                for at, term in terms.items():
                    add(slot, at, term)

        @pl.when(self.core == 0)
        def _():
            rows(BEFORE, self.before[1], 0)

        @pl.when(self.core == 1)
        def _():
            rows(AFTER, self.after[1], ny)

    def dz(self, comp, x):
        slot = [c for c, _ in self.spec[2]].index(comp)
        return self.edges[slot, x * self.ny : (x + 1) * self.ny, :]


def pack(spec, fields, core, own, given):
    nx, ny, nz = fields.shape[1:]
    row = lax.broadcasted_iota(jnp.int32, (16, nz), 0)
    lane = lax.broadcasted_iota(jnp.int32, (16, nz), 1)
    before, after = layers(spec[2], BEFORE), layers(spec[2], AFTER)
    total = None
    for comp, _ in spec[2]:
        pick = jnp.zeros((16, nz), jnp.float32)
        for i, (c, off) in enumerate(before):
            if c == comp:
                pick = jnp.where((row == i) & (lane == nz + off), 1.0, pick)
        for i, (c, off) in enumerate(after):
            if c == comp:
                pick = jnp.where((row == 8 + i) & (lane == off), 1.0, pick)
        pick = pick.astype(jnp.bfloat16)
        for third in thirds(fields[comp].reshape(nx * ny, nz)):
            part = lax.dot_general(
                pick, third, (((1,), (1,)), ((), ())), preferred_element_type=jnp.float32
            )
            total = part if total is None else total + part
    half = nx * ny // 2
    ends = [jnp.concatenate([t[:, :half], t[:, half:]], axis=0) for t in (total[:8], total[8:])]

    def write(up, down, inner_up):
        for ref, sides in ((up, BEFORE), (down, AFTER)):
            for i, (comp, off) in enumerate(layers(spec[0], sides)):
                ref[i] = fields[comp, nx + off if sides is BEFORE else off]
        up[FACE] = ends[0]
        down[FACE] = ends[1]
        inner, outer = (BEFORE, AFTER) if inner_up else (AFTER, BEFORE)
        for ref, sides in ((given, inner), (own, outer)):
            for i, (comp, off) in enumerate(layers(spec[1], sides)):
                ref[INNER + i] = fields[comp, :, ny + off if sides is BEFORE else off, :]

    @pl.when(core == 0)
    def _():
        write(own, given, True)

    @pl.when(core == 1)
    def _():
        write(given, own, False)


def first_kernel(core, stress, own, given):
    pack(STRESS, stress, core[0], own, given)


def gather_kernel(core, own, pair, along_x, along_y, along_z):
    here = core[0]
    there = 1 - here
    other = there * GIVEN
    along_x[pl.ds(here * FACE, FACE)] = own[:FACE]
    along_x[pl.ds(there * FACE, FACE)] = pair[pl.ds(other, FACE)]
    along_z[here] = own[FACE]
    along_z[there] = pair[other + FACE]
    along_y[...] = own[INNER:]


def join_kernel(along_x, along_z, near, taken):
    taken[: 2 * FACE] = along_x[...]
    taken[2 * FACE :] = along_z[...]


def cells_kernel(first, table, mech, weight, top, behind, decay, gain, limits):
    limits[...] = (top[...] - first[0]).astype(jnp.float32).T
    for x in range(mech.shape[0]):
        here = jnp.zeros(mech.shape[1:], jnp.float32)
        for level in range(table.shape[0]):
            here = jnp.where(mech[x] == level, table[level], here)
        decay[x] = here
        gain[x] = (1.0 - here) * weight[x]


def near_velocity_kernel(core, stress, velocity, buoyancy, pair, behind, out, rows):
    near = Near(STRESS, stress, core[0], pair, rows)
    for x in range(velocity.shape[1]):
        scale = TIME_STEP * buoyancy[x]
        out[0, x] = velocity[0, x] + scale * (near.dx(0, x) + near.dy(3, x) + near.dz(4, x))
        out[1, x] = velocity[1, x] + scale * (near.dx(3, x) + near.dy(1, x) + near.dz(5, x))
        out[2, x] = velocity[2, x] + scale * (near.dx(4, x) + near.dy(5, x) + near.dz(2, x))


def velocity_kernel(core, near, buoyancy, spread, outer, out, own, given, edges):
    far = Far(STRESS, near.shape[1:], core[0], spread, edges)
    for x in range(near.shape[1]):
        scale = TIME_STEP * buoyancy[x]
        out[0, x] = near[0, x] + scale * (far.dx(0, x) + far.dz(4, x))
        out[1, x] = near[1, x] + scale * (far.dx(3, x) + far.dz(5, x))
        out[2, x] = near[2, x] + scale * (far.dx(4, x) + far.dz(2, x))

    def add(slot, row, terms):
        out[slot, :, row, :] = out[slot, :, row, :] + TIME_STEP * buoyancy[:, row, :] * terms

    far.outer_rows(outer, add)
    pack(VELOCITY, out, core[0], own, given)


def near_strain_kernel(core, velocity, pair, behind, out, rows):
    near = Near(VELOCITY, velocity, core[0], pair, rows)
    for x in range(velocity.shape[1]):
        out[0, x] = near.dx(0, x)
        out[1, x] = near.dy(1, x)
        out[2, x] = near.dz(2, x)
        out[3, x] = near.dy(0, x) + near.dx(1, x)
        out[4, x] = near.dz(0, x) + near.dx(2, x)
        out[5, x] = near.dz(1, x) + near.dy(2, x)


def stress_kernel(send, core, near, stress, memory, lam, shear, decay, gain, limits, *refs):
    if send:
        spread, outer, out, kept, own, given, edges, rows = refs
    else:
        spread, outer, *finals, out, kept, sems, edges, rows = refs
    nx, ny, nz = lam.shape
    far = Far(VELOCITY, lam.shape, core[0], spread, edges)
    depth = lax.broadcasted_iota(jnp.int32, (1, nz), 1).astype(jnp.float32)
    rows[...] = jnp.zeros(rows.shape, jnp.float32)

    def add(slot, row, terms):
        rows[slot, :, row, :] = terms

    far.outer_rows(outer, add)
    copies = []
    for x in range(nx):
        top = limits[:, x : x + 1]
        solid = depth >= top
        below = depth > top
        xx, yy, zz = near[0, x] + far.dx(0, x), near[1, x] + rows[0, x], near[2, x] + far.dz(2, x)
        volume = lam[x] * (xx + yy + zz)
        double = 2.0 * shear[x]
        rates = (
            volume + double * xx,
            volume + double * yy,
            volume + double * zz,
            shear[x] * (near[3, x] + rows[1, x] + far.dx(1, x)),
            shear[x] * (near[4, x] + far.dz(0, x) + far.dx(2, x)),
            shear[x] * (near[5, x] + rows[2, x] + far.dz(1, x)),
        )
        for comp, rate in enumerate(rates):
            new = decay[x] * memory[comp, x] + gain[x] * rate
            kept[comp, x] = new
            keep = below if comp in (2, 4, 5) else solid
            out[comp, x] = jnp.where(keep, stress[comp, x] + TIME_STEP * (rate - new), 0.0)
        size = nx // GROUPS
        if not send and (x + 1) % size == 0:
            part = pl.ds(x + 1 - size, size)
            for i, (held, final) in enumerate(zip((out, kept), finals)):
                copy = pltpu.make_async_copy(
                    held.at[:, part], final.at[:, part], sems.at[i, x // size]
                )
                copy.start()
                copies.append(copy)
    for copy in copies:
        copy.wait()
    if send:
        pack(STRESS, out, core[0], own, given)


def call(body, outs, operands, scalars=1, scratch=(), hold=False, out_space=pltpu.VMEM):
    vmem = pl.BlockSpec(memory_space=pltpu.VMEM)
    specs = [pl.BlockSpec(memory_space=pltpu.SMEM)] * scalars
    specs += [vmem] * (len(operands) - scalars)
    if hold:
        specs[-1] = pl.BlockSpec(memory_space=pl.ANY)
    return pl.pallas_call(
        body,
        out_shape=outs,
        in_specs=specs,
        out_specs=[pl.BlockSpec(memory_space=out_space)] * len(outs),
        scratch_shapes=list(scratch),
        cost_estimate=pl.CostEstimate(flops=2**22, bytes_accessed=2**22, transcendentals=0)
        if hold
        else None,
        compiler_params=pltpu.CompilerParams(vmem_limit_bytes=24 * 1024 * 1024),
    )(*operands)


def exchange(core, own, given, near_kernel):
    plane = own.shape[1:]
    planes = lambda n: jax.ShapeDtypeStruct((n,) + plane, own.dtype)
    gx, gy, gz = [lax.axis_size(axis) for axis in AXES]
    cores = [[j, j + 1] for j in range(0, gy, 2)]
    pair = lax.all_gather(given, "gy", axis=0, tiled=True, axis_index_groups=cores)
    along_x, along_y, along_z = call(
        gather_kernel, [planes(2 * FACE), planes(FACE), planes(2)], [core, own, pair]
    )
    to_x, to_z = [], []
    for j in range(gy):
        step = 1 - 2 * (j % 2)
        to_x += [(i * gy + j, (i + step) * gy + j) for i in range(gx) if 0 <= i + step < gx]
        to_z += [(j * gz + k, j * gz + k + step) for k in range(gz) if 0 <= k + step < gz]
    to_y = [(j, j + 1) for j in range(1, gy - 1, 2)] + [(j + 1, j) for j in range(1, gy - 1, 2)]
    got_x = lax.ppermute(along_x, ("gx", "gy"), to_x)
    got_z = lax.ppermute(along_z, ("gy", "gz"), to_z)
    outer = lax.ppermute(along_y, "gy", to_y)
    near = near_kernel(pair, along_x)
    (taken,) = call(join_kernel, [planes(TAKEN)], [got_x, got_z, near], scalars=0, hold=True)
    spread = lax.all_gather(taken, "gy", axis=0, tiled=True, axis_index_groups=cores)
    return near, spread, outer, along_x


def shards(
    velocity,
    stress,
    memory,
    lame_lambda,
    shear_modulus,
    buoyancy,
    anelastic_weight,
    decay_table,
    mech_index,
    surface_depth,
):
    nx, ny, nz = lame_lambda.shape
    core = (lax.axis_index("gy") % 2).astype(jnp.int32).reshape(1)
    first = (lax.axis_index("gz") * nz).astype(jnp.int32).reshape(1)
    like = lambda a: jax.ShapeDtypeStruct(a.shape, jnp.float32)
    packed = [jax.ShapeDtypeStruct((GIVEN, ny, nz), jnp.float32)] * 2
    rows = [pltpu.VMEM((3, nx, ny + 16, nz), jnp.float32)]
    edges = [pltpu.VMEM((3, nx * ny, nz), jnp.float32)]
    terms = [pltpu.VMEM((3, nx, ny, nz), jnp.float32)]
    held = [
        pltpu.VMEM(stress.shape, jnp.float32),
        pltpu.VMEM(memory.shape, jnp.float32),
        pltpu.SemaphoreType.DMA((2, GROUPS)),
    ]
    own, given = call(first_kernel, packed, [core, stress])
    for step in range(STEPS):

        def near_velocity(*got):
            operands = [core, stress, velocity, buoyancy, *got]
            outs = [like(velocity)]
            return call(near_velocity_kernel, outs, operands, scratch=rows, hold=True)[0]

        def near_strain(*got):
            outs = [like(stress)]
            return call(near_strain_kernel, outs, [core, velocity, *got], scratch=rows, hold=True)[0]

        near, spread, outer, along = exchange(core, own, given, near_velocity)
        if step == 0:
            cells = call(
                cells_kernel,
                [like(lame_lambda)] * 2 + [like(surface_depth)],
                [first, decay_table, mech_index, anelastic_weight, surface_depth, along],
                scalars=2,
                hold=True,
            )
        velocity, own, given = call(
            velocity_kernel,
            [like(velocity)] + packed,
            [core, near, buoyancy, spread, outer],
            scratch=edges,
        )
        near, spread, outer, _ = exchange(core, own, given, near_strain)
        send = step < STEPS - 1
        stress, memory, *rest = call(
            functools.partial(stress_kernel, send),
            [like(stress), like(memory)] + (packed if send else []),
            [core, near, stress, memory, lame_lambda, shear_modulus, *cells, spread, outer],
            scratch=(edges if send else held + edges) + terms,
            out_space=pltpu.VMEM if send else pl.ANY,
        )
        if send:
            own, given = rest
    return (velocity, stress, memory)


def solution(mesh):
    fields = P(None, *AXES)
    cells = P(*AXES)
    return jax.shard_map(
        shards,
        mesh=mesh,
        in_specs=(fields,) * 3 + (cells,) * 4 + (P(), cells, P("gx", "gy")),
        out_specs=(fields,) * 3,
        check_vma=False,
    )
```

```python
import functools

import jax
import jax.numpy as jnp
from jax import lax
from jax.experimental import pallas as pl
from jax.experimental.pallas import tpu as pltpu
from jax.sharding import PartitionSpec as P

STEPS = 2
COEF_NEAR = 9.0 / 8.0
COEF_FAR = -1.0 / 24.0
TIME_STEP = 0.2
AXES = ("gx", "gy", "gz")

STRESS = (
    ((0, "f"), (3, "b"), (4, "b")),
    ((3, "b"), (1, "f"), (5, "b")),
    ((4, "b"), (5, "b"), (2, "f")),
)
VELOCITY = (
    ((0, "b"), (1, "f"), (2, "f")),
    ((1, "b"), (0, "f"), (2, "f")),
    ((2, "b"), (0, "f"), (1, "f")),
)
BEFORE = {"f": (-1,), "b": (-2, -1)}
AFTER = {"f": (0, 1), "b": (0,)}
TAPS = {
    "f": ((1, COEF_NEAR), (0, -COEF_NEAR), (2, COEF_FAR), (-1, -COEF_FAR)),
    "b": ((0, COEF_NEAR), (-1, -COEF_NEAR), (1, COEF_FAR), (-2, -COEF_FAR)),
}

GROUPS = 4
FACE = 5
INNER = FACE + 1
GIVEN = INNER + FACE
TAKEN = 2 * FACE + 2


def layers(spec, sides):
    return [(comp, off) for comp, kind in spec for off in sides[kind]]


def weighted(taps):
    a, b, c, d = taps
    return COEF_NEAR * (a - b) + COEF_FAR * (c - d)


def thirds(value):
    high = value.astype(jnp.bfloat16)
    rest = value - high.astype(jnp.float32)
    middle = rest.astype(jnp.bfloat16)
    return high, middle, (rest - middle.astype(jnp.float32)).astype(jnp.bfloat16)


class Near:
    def __init__(self, spec, fields, core, pair, rows):
        self.spec, self.fields, self.rows = spec, fields, rows
        self.nx, self.ny, self.nz = nx, ny, nz = fields.shape[1:]
        first = {k: i for i, k in enumerate(layers(spec[1], BEFORE))}
        last = {k: i for i, k in enumerate(layers(spec[1], AFTER))}
        for slot, (comp, kind) in enumerate(spec[1]):
            for x in range(nx):
                rows[slot, x, 8 : 8 + ny, :] = fields[comp, x]

        def beside(before, after):
            for slot, (comp, kind) in enumerate(spec[1]):
                for x in range(nx):
                    for off in BEFORE[kind]:
                        rows[slot, x, 8 + off : 9 + off, :] = before(first[comp, off], x)
                    for off in AFTER[kind]:
                        rows[slot, x, 8 + ny + off : 9 + ny + off, :] = after(last[comp, off], x)

        beyond = lambda i, x: jnp.zeros((1, nz), jnp.float32)

        @pl.when(core == 0)
        def _():
            beside(beyond, lambda i, x: pair[GIVEN + INNER + i, x : x + 1, :])

        @pl.when(core == 1)
        def _():
            beside(lambda i, x: pair[INNER + i, x : x + 1, :], beyond)

    def dx(self, comp, x):
        taps = TAPS[dict(self.spec[0])[comp]]
        if all(0 <= x + off < self.nx for off, _ in taps):
            return weighted([self.fields[comp, x + off] for off, _ in taps])
        return sum(w * self.fields[comp, x + off] for off, w in taps if 0 <= x + off < self.nx)

    def dy(self, comp, x):
        slot = [c for c, _ in self.spec[1]].index(comp)
        kind = self.spec[1][slot][1]
        return weighted(
            [self.rows[slot, x, 8 + off : 8 + off + self.ny, :] for off, _ in TAPS[kind]]
        )

    def dz(self, comp, x):
        here = self.fields[comp, x]
        lane = lax.broadcasted_iota(jnp.int32, (1, self.nz), 1)
        total = None
        for off, weight in TAPS[dict(self.spec[2])[comp]]:
            if off == 0:
                term = weight * here
            else:
                inside = (lane + off >= 0) & (lane + off < self.nz)
                term = jnp.where(inside, weight, 0.0) * pltpu.roll(here, (-off) % self.nz, 1)
            total = term if total is None else total + term
        return total


class Far:
    def __init__(self, spec, shape, core, spread, edges):
        self.spec, self.core, self.spread, self.edges = spec, core, spread, edges
        self.nx, self.ny, self.nz = nx, ny, nz = shape
        self.before = [{k: i for i, k in enumerate(layers(s, BEFORE))} for s in spec]
        self.after = [{k: i for i, k in enumerate(layers(s, AFTER))} for s in spec]
        ends = [spread[side * TAKEN + 2 * FACE + core] for side in (0, 1)]
        got = jnp.concatenate([jnp.concatenate([e[:8], e[8:]], axis=1) for e in ends], axis=0)
        row = lax.broadcasted_iota(jnp.int32, (16, nz), 0)
        lane = lax.broadcasted_iota(jnp.int32, (16, nz), 1)
        weights = []
        for comp, kind in spec[2]:
            here = jnp.zeros((16, nz), jnp.float32)
            for shift, weight in TAPS[kind]:
                scaled = float(round(24 * weight))
                places = [(self.before[2][comp, off], off - shift) for off in BEFORE[kind]]
                places += [(8 + self.after[2][comp, off], nz + off - shift) for off in AFTER[kind]]
                for i, at in places:
                    if 0 <= at < nz:
                        here = jnp.where((row == i) & (lane == at), scaled, here)
            weights.append(here)
        weights = jnp.concatenate(weights, axis=1).astype(jnp.bfloat16)
        weights = jnp.concatenate([weights] * 3, axis=0)
        stacked = jnp.concatenate([p.astype(jnp.float32) for p in thirds(got)], axis=0).T
        total = jnp.dot(stacked.astype(jnp.bfloat16), weights, preferred_element_type=jnp.float32)
        for slot in range(3):
            edges[slot] = total[:, slot * nz : (slot + 1) * nz] * (1.0 / 24.0)

    def dx(self, comp, x):
        total = 0.0
        for off, weight in TAPS[dict(self.spec[0])[comp]]:
            at = x + off
            if at < 0:
                here = self.spread[self.core * FACE + self.before[0][comp, at]]
                total = total + weight * here
            elif at >= self.nx:
                i = self.after[0][comp, at - self.nx]
                total = total + weight * self.spread[TAKEN + self.core * FACE + i]
        return total

    def outer_rows(self, outer, add):
        ny = self.ny

        def rows(sides, place, base):
            for slot, (comp, kind) in enumerate(self.spec[1]):
                terms = {}
                for off in sides[kind]:
                    for shift, weight in TAPS[kind]:
                        at = base + off - shift
                        if 0 <= at < ny:
                            term = weight * outer[place[comp, off]]
                            terms[at] = terms[at] + term if at in terms else term
                for at, term in terms.items():
                    add(slot, at, term)

        @pl.when(self.core == 0)
        def _():
            rows(BEFORE, self.before[1], 0)

        @pl.when(self.core == 1)
        def _():
            rows(AFTER, self.after[1], ny)

    def dz(self, comp, x):
        slot = [c for c, _ in self.spec[2]].index(comp)
        return self.edges[slot, x * self.ny : (x + 1) * self.ny, :]


def pack(spec, fields, core, own, given):
    nx, ny, nz = fields.shape[1:]
    row = lax.broadcasted_iota(jnp.int32, (16, nz), 0)
    lane = lax.broadcasted_iota(jnp.int32, (16, nz), 1)
    before, after = layers(spec[2], BEFORE), layers(spec[2], AFTER)
    total = None
    for comp, _ in spec[2]:
        pick = jnp.zeros((16, nz), jnp.float32)
        for i, (c, off) in enumerate(before):
            if c == comp:
                pick = jnp.where((row == i) & (lane == nz + off), 1.0, pick)
        for i, (c, off) in enumerate(after):
            if c == comp:
                pick = jnp.where((row == 8 + i) & (lane == off), 1.0, pick)
        pick = pick.astype(jnp.bfloat16)
        for third in thirds(fields[comp].reshape(nx * ny, nz)):
            part = lax.dot_general(
                pick, third, (((1,), (1,)), ((), ())), preferred_element_type=jnp.float32
            )
            total = part if total is None else total + part
    half = nx * ny // 2
    ends = [jnp.concatenate([t[:, :half], t[:, half:]], axis=0) for t in (total[:8], total[8:])]

    def write(up, down, inner_up):
        for ref, sides in ((up, BEFORE), (down, AFTER)):
            for i, (comp, off) in enumerate(layers(spec[0], sides)):
                ref[i] = fields[comp, nx + off if sides is BEFORE else off]
        up[FACE] = ends[0]
        down[FACE] = ends[1]
        inner, outer = (BEFORE, AFTER) if inner_up else (AFTER, BEFORE)
        for ref, sides in ((given, inner), (own, outer)):
            for i, (comp, off) in enumerate(layers(spec[1], sides)):
                ref[INNER + i] = fields[comp, :, ny + off if sides is BEFORE else off, :]

    @pl.when(core == 0)
    def _():
        write(own, given, True)

    @pl.when(core == 1)
    def _():
        write(given, own, False)


def first_kernel(core, stress, own, given):
    pack(STRESS, stress, core[0], own, given)


def gather_kernel(core, own, pair, along_x, along_y, along_z):
    here = core[0]
    there = 1 - here
    other = there * GIVEN
    along_x[pl.ds(here * FACE, FACE)] = own[:FACE]
    along_x[pl.ds(there * FACE, FACE)] = pair[pl.ds(other, FACE)]
    along_z[here] = own[FACE]
    along_z[there] = pair[other + FACE]
    along_y[...] = own[INNER:]


def join_kernel(along_x, along_z, near, taken):
    taken[: 2 * FACE] = along_x[...]
    taken[2 * FACE :] = along_z[...]


def cells_kernel(first, table, mech, weight, top, behind, decay, gain, limits):
    limits[...] = (top[...] - first[0]).astype(jnp.float32).T
    for x in range(mech.shape[0]):
        here = jnp.zeros(mech.shape[1:], jnp.float32)
        for level in range(table.shape[0]):
            here = jnp.where(mech[x] == level, table[level], here)
        decay[x] = here
        gain[x] = (1.0 - here) * weight[x]


def near_velocity_kernel(core, stress, velocity, buoyancy, pair, behind, out, rows):
    near = Near(STRESS, stress, core[0], pair, rows)
    for x in range(velocity.shape[1]):
        scale = TIME_STEP * buoyancy[x]
        out[0, x] = velocity[0, x] + scale * (near.dx(0, x) + near.dy(3, x) + near.dz(4, x))
        out[1, x] = velocity[1, x] + scale * (near.dx(3, x) + near.dy(1, x) + near.dz(5, x))
        out[2, x] = velocity[2, x] + scale * (near.dx(4, x) + near.dy(5, x) + near.dz(2, x))


def velocity_kernel(core, near, buoyancy, spread, outer, out, own, given, edges):
    far = Far(STRESS, near.shape[1:], core[0], spread, edges)
    for x in range(near.shape[1]):
        scale = TIME_STEP * buoyancy[x]
        out[0, x] = near[0, x] + scale * (far.dx(0, x) + far.dz(4, x))
        out[1, x] = near[1, x] + scale * (far.dx(3, x) + far.dz(5, x))
        out[2, x] = near[2, x] + scale * (far.dx(4, x) + far.dz(2, x))

    def add(slot, row, terms):
        out[slot, :, row, :] = out[slot, :, row, :] + TIME_STEP * buoyancy[:, row, :] * terms

    far.outer_rows(outer, add)
    pack(VELOCITY, out, core[0], own, given)


def near_strain_kernel(core, velocity, pair, behind, out, *refs):
    *final, rows = refs
    if final:
        copy = pltpu.make_async_copy(velocity, final[0], final[1].at[0])
        copy.start()
    near = Near(VELOCITY, velocity, core[0], pair, rows)
    for x in range(velocity.shape[1]):
        out[0, x] = near.dx(0, x)
        out[1, x] = near.dy(1, x)
        out[2, x] = near.dz(2, x)
        out[3, x] = near.dy(0, x) + near.dx(1, x)
        out[4, x] = near.dz(0, x) + near.dx(2, x)
        out[5, x] = near.dz(1, x) + near.dy(2, x)
    if final:
        copy.wait()


def stress_kernel(send, core, near, stress, memory, lam, shear, decay, gain, limits, *refs):
    if send:
        spread, outer, out, kept, own, given, edges, rows = refs
    else:
        spread, outer, *finals, out, kept, sems, edges, rows = refs
    nx, ny, nz = lam.shape
    far = Far(VELOCITY, lam.shape, core[0], spread, edges)
    depth = lax.broadcasted_iota(jnp.int32, (1, nz), 1).astype(jnp.float32)
    rows[...] = jnp.zeros(rows.shape, jnp.float32)

    def add(slot, row, terms):
        rows[slot, :, row, :] = terms

    far.outer_rows(outer, add)
    copies = []
    for x in range(nx):
        top = limits[:, x : x + 1]
        solid = depth >= top
        below = depth > top
        xx, yy, zz = near[0, x] + far.dx(0, x), near[1, x] + rows[0, x], near[2, x] + far.dz(2, x)
        volume = lam[x] * (xx + yy + zz)
        double = 2.0 * shear[x]
        rates = (
            volume + double * xx,
            volume + double * yy,
            volume + double * zz,
            shear[x] * (near[3, x] + rows[1, x] + far.dx(1, x)),
            shear[x] * (near[4, x] + far.dz(0, x) + far.dx(2, x)),
            shear[x] * (near[5, x] + rows[2, x] + far.dz(1, x)),
        )
        for comp, rate in enumerate(rates):
            new = decay[x] * memory[comp, x] + gain[x] * rate
            kept[comp, x] = new
            keep = below if comp in (2, 4, 5) else solid
            out[comp, x] = jnp.where(keep, stress[comp, x] + TIME_STEP * (rate - new), 0.0)
        size = nx // GROUPS
        if not send and (x + 1) % size == 0:
            part = pl.ds(x + 1 - size, size)
            for i, (held, final) in enumerate(zip((out, kept), finals)):
                copy = pltpu.make_async_copy(
                    held.at[:, part], final.at[:, part], sems.at[i, x // size]
                )
                copy.start()
                copies.append(copy)
    for copy in copies:
        copy.wait()
    if send:
        pack(STRESS, out, core[0], own, given)


def call(body, outs, operands, scalars=1, scratch=(), hold=False, out_space=None):
    vmem = pl.BlockSpec(memory_space=pltpu.VMEM)
    specs = [pl.BlockSpec(memory_space=pltpu.SMEM)] * scalars
    specs += [vmem] * (len(operands) - scalars)
    if hold:
        specs[-1] = pl.BlockSpec(memory_space=pl.ANY)
    return pl.pallas_call(
        body,
        out_shape=outs,
        in_specs=specs,
        out_specs=[pl.BlockSpec(memory_space=s) for s in out_space or [pltpu.VMEM] * len(outs)],
        scratch_shapes=list(scratch),
        cost_estimate=pl.CostEstimate(flops=2**22, bytes_accessed=2**22, transcendentals=0)
        if hold
        else None,
        compiler_params=pltpu.CompilerParams(vmem_limit_bytes=24 * 1024 * 1024),
    )(*operands)


def exchange(core, own, given, near_kernel):
    plane = own.shape[1:]
    planes = lambda n: jax.ShapeDtypeStruct((n,) + plane, own.dtype)
    gx, gy, gz = [lax.axis_size(axis) for axis in AXES]
    cores = [[j, j + 1] for j in range(0, gy, 2)]
    pair = lax.all_gather(given, "gy", axis=0, tiled=True, axis_index_groups=cores)
    along_x, along_y, along_z = call(
        gather_kernel, [planes(2 * FACE), planes(FACE), planes(2)], [core, own, pair]
    )
    to_x, to_z = [], []
    for j in range(gy):
        step = 1 - 2 * (j % 2)
        to_x += [(i * gy + j, (i + step) * gy + j) for i in range(gx) if 0 <= i + step < gx]
        to_z += [(j * gz + k, j * gz + k + step) for k in range(gz) if 0 <= k + step < gz]
    to_y = [(j, j + 1) for j in range(1, gy - 1, 2)] + [(j + 1, j) for j in range(1, gy - 1, 2)]
    got_x = lax.ppermute(along_x, ("gx", "gy"), to_x)
    got_z = lax.ppermute(along_z, ("gy", "gz"), to_z)
    outer = lax.ppermute(along_y, "gy", to_y)
    near, *rest = near_kernel(pair, along_x)
    (taken,) = call(join_kernel, [planes(TAKEN)], [got_x, got_z, near], scalars=0, hold=True)
    spread = lax.all_gather(taken, "gy", axis=0, tiled=True, axis_index_groups=cores)
    return near, spread, outer, along_x, rest


def shards(
    velocity,
    stress,
    memory,
    lame_lambda,
    shear_modulus,
    buoyancy,
    anelastic_weight,
    decay_table,
    mech_index,
    surface_depth,
):
    nx, ny, nz = lame_lambda.shape
    core = (lax.axis_index("gy") % 2).astype(jnp.int32).reshape(1)
    first = (lax.axis_index("gz") * nz).astype(jnp.int32).reshape(1)
    like = lambda a: jax.ShapeDtypeStruct(a.shape, jnp.float32)
    packed = [jax.ShapeDtypeStruct((GIVEN, ny, nz), jnp.float32)] * 2
    rows = [pltpu.VMEM((3, nx, ny + 16, nz), jnp.float32)]
    edges = [pltpu.VMEM((3, nx * ny, nz), jnp.float32)]
    terms = [pltpu.VMEM((3, nx, ny, nz), jnp.float32)]
    held = [
        pltpu.VMEM(stress.shape, jnp.float32),
        pltpu.VMEM(memory.shape, jnp.float32),
        pltpu.SemaphoreType.DMA((2, GROUPS)),
    ]
    own, given = call(first_kernel, packed, [core, stress])
    for step in range(STEPS):

        def near_velocity(*got):
            operands = [core, stress, velocity, buoyancy, *got]
            outs = [like(velocity)]
            return call(near_velocity_kernel, outs, operands, scratch=rows, hold=True)

        def near_strain(*got):
            last = step == STEPS - 1
            return call(
                near_strain_kernel,
                [like(stress), like(velocity)] if last else [like(stress)],
                [core, velocity, *got],
                scratch=[pltpu.SemaphoreType.DMA((1,))] + rows if last else rows,
                hold=True,
                out_space=[pltpu.VMEM, pl.ANY] if last else None,
            )

        near, spread, outer, along, _ = exchange(core, own, given, near_velocity)
        if step == 0:
            cells = call(
                cells_kernel,
                [like(lame_lambda)] * 2 + [like(surface_depth)],
                [first, decay_table, mech_index, anelastic_weight, surface_depth, along],
                scalars=2,
                hold=True,
            )
        velocity, own, given = call(
            velocity_kernel,
            [like(velocity)] + packed,
            [core, near, buoyancy, spread, outer],
            scratch=edges,
        )
        near, spread, outer, _, final = exchange(core, own, given, near_strain)
        send = step < STEPS - 1
        stress, memory, *rest = call(
            functools.partial(stress_kernel, send),
            [like(stress), like(memory)] + (packed if send else []),
            [core, near, stress, memory, lame_lambda, shear_modulus, *cells, spread, outer],
            scratch=(edges if send else held + edges) + terms,
            out_space=None if send else [pl.ANY] * 2,
        )
        if send:
            own, given = rest
    return (final[0], stress, memory)


def solution(mesh):
    fields = P(None, *AXES)
    cells = P(*AXES)
    return jax.shard_map(
        shards,
        mesh=mesh,
        in_specs=(fields,) * 3 + (cells,) * 4 + (P(), cells, P("gx", "gy")),
        out_specs=(fields,) * 3,
        check_vma=False,
    )
```
